128 devices in a mesh: dp: 8 (over y_hi, x), ctx: 16 (over z, y_lo, core).
Axes of the slice: x: 4, y: 4 (y_hi: 2, y_lo: 2; y = y_hi * 2 + y_lo), z: 4, core: 2. Of those that a mesh axis runs over, the one named last changes fastest.
Arguments:
- query: bfloat16 [8, 2048, 4096], P('dp', 'ctx'), may hold values from -6 to 6
- key: bfloat16 [8, 2048, 256], P('dp', 'ctx'), may hold values from -6 to 6
- value: bfloat16 [8, 2048, 256], P('dp', 'ctx'), may hold values from -6 to 6
- span_order: int32 [8, 32], P('dp'), may hold values from 0 to 31, each once within a row
- expert_ids: int32 [8, 2048, 8], P('dp', 'ctx'), may hold values from 0 to 127, as said below
- expert_gates: float32 [8, 2048, 8], P('dp', 'ctx'), may hold values from 0.02 to 0.2
- trainable: int32 [16], replicated, may hold values from 0 to 127, as said below
- norm_gain: float32 [4096], replicated, may hold values from 0.5 to 1.5
- upstream: bfloat16 [8, 2048, 4096], P('dp', 'ctx'), may hold values from -6 to 6
- expert_weights: bfloat16 [16, 768, 3, 4096], P('ctx'), may hold values from -0.09375 to 0.09375
Outputs:
- d_query: bfloat16 [8, 2048, 4096], P('dp', 'ctx')
- key_gradient: bfloat16 [8, 2048, 256], P('dp', 'ctx')
- value_gradient: bfloat16 [8, 2048, 256], P('dp', 'ctx')
- expert_grads: bfloat16 [16, 768, 3, 4096], P('ctx', 'dp')
The draws below stay inside these ranges and needn't reach their ends.
Inputs may be any that keep to these rules, and one draw needn't show every extreme that they name: `span_order`: each row is a permutation of the 32 span numbers. `expert_ids`: the 8 numbers of a token are distinct; among the 128 rows of one device (aligned blocks of 128 rows of a document) at most 12 name the same expert. `trainable`: distinct expert numbers.
All inputs are finite; a program needn't handle non-finite values.
Results may differ from the reference program's by a relative error of at most 0.02.
Values may be sent and summed in bfloat16 or wider, within the bound.
A program may use at most 128 MiB of HBM per device.

```python
import math
import jax
import jax.numpy as jnp
from jax import lax

D = 4096
QUERY_HEADS = 32
KEY_VALUE_HEADS = 2
HEAD_SIZE = 128
H = 768
EXPERTS = 128
TOP = 8
TOK_DEV = 128
TRAIN = 16
DOCUMENT_LENGTH = 2048
CAP = 12
N_DP = 8
N_CTX = 16


def drawn_fields(base_key):
    seed_all = jax.random.fold_in(base_key, 11)
    key_query, key_random_keys = jax.random.split(seed_all, 2)
    query_vals = jnp.clip(jax.random.normal(key_query, (N_DP, DOCUMENT_LENGTH, QUERY_HEADS * HEAD_SIZE), jnp.float32), -5.5, 5.5)
    key_entries = jnp.clip(jax.random.normal(key_random_keys, (N_DP, DOCUMENT_LENGTH, KEY_VALUE_HEADS * HEAD_SIZE), jnp.float32), -5.5, 5.5)
    return (query_vals, key_entries)


def routing_tables(base_key):
    seed_all = jax.random.fold_in(base_key, 29)
    key_pick, key_full, key_level, key_noise, key_row_block = jax.random.split(seed_all, 5)
    trainable = jax.random.permutation(key_pick, EXPERTS)[:TRAIN].astype(jnp.int32)
    full_slot = jax.random.randint(key_full, (), 0, TRAIN)
    full_expert = jnp.sum(jnp.where(jnp.arange(TRAIN) == full_slot, trainable, 0))
    expert_num = jnp.arange(EXPERTS, dtype=jnp.int32)
    levels = jax.random.randint(key_level, (EXPERTS,), 0, 4)
    levels = jnp.where(expert_num == full_expert, 8, levels)
    block_count = N_DP * N_CTX
    entries = EXPERTS * CAP
    entry_num = jnp.arange(entries, dtype=jnp.int32)
    owner_of = entry_num // CAP
    noise_vals = jax.random.randint(key_noise, (block_count, entries), 0, 4096)
    priority = (levels[owner_of][None, :] * 4096 + noise_vals) * entries + entry_num[None, :]
    assigned = TOK_DEV * TOP
    kept_idx = jnp.sort(jnp.argsort(-priority, axis=1)[:, :assigned], axis=1)
    chosen = (kept_idx // CAP).astype(jnp.int32)
    id_table = chosen.reshape(block_count, TOP, TOK_DEV).transpose(0, 2, 1)
    shuffle = jax.random.randint(key_row_block, (block_count, TOK_DEV), 0, 4096) * TOK_DEV + jnp.arange(TOK_DEV)[None, :]
    row_perm = jnp.argsort(shuffle, axis=1)
    id_table = jnp.take_along_axis(id_table, row_perm[:, :, None], axis=1)
    return (trainable, id_table.reshape(N_DP, DOCUMENT_LENGTH, TOP).astype(jnp.int32))


def draw_query(key, part):
    return drawn_fields(key)[0].astype(jnp.bfloat16)


def draw_key(key, part):
    return drawn_fields(key)[1].astype(jnp.bfloat16)


def draw_expert_ids(key, part):
    return routing_tables(key)[1]


def draw_trainable(key, part):
    return routing_tables(key)[0]


def steps_of(rng, shape, cuts, low, high):
    def one(dim, blocks):
        steps = jax.random.uniform(jax.random.fold_in(jax.random.fold_in(rng, 6), dim), (blocks,), jnp.float32, low / len(cuts), high / len(cuts))
        return jnp.repeat(jnp.exp(steps), shape[dim] // blocks).reshape((-1,) + (1,) * (len(shape) - dim - 1))

    loudness = one(*cuts[0])
    for cut in cuts[1:]:
        loudness = loudness * one(*cut)
    return loudness


def gaussian(own_key, dims, deviation, reach, cuts=(), held_as=jnp.bfloat16):
    values = deviation * jax.random.normal(own_key, dims, jnp.float32)
    if cuts:
        values = values * steps_of(own_key, dims, cuts, -0.22, 0.18)
    return jnp.clip(values, -reach, reach).astype(held_as)


def setup_inputs(seed: int = 0) -> dict:
    arg_keys = jax.random.split(jax.random.key(seed), 11)
    return {
        "query": draw_query(jax.random.fold_in(arg_keys[10], 71), 0),
        "key": draw_key(jax.random.fold_in(arg_keys[10], 71), 0),
        "value": gaussian(arg_keys[2], (N_DP, DOCUMENT_LENGTH, KEY_VALUE_HEADS * HEAD_SIZE), 1.0, 6.0, ((0, 8), (1, 16))),
        "span_order": jax.vmap(lambda own: jax.random.permutation(own, 2 * N_CTX))(jax.random.split(arg_keys[3], N_DP)).reshape((N_DP, 2 * N_CTX)).astype(jnp.int32),
        "expert_ids": draw_expert_ids(jax.random.fold_in(arg_keys[10], 71), 0),
        "expert_gates": jnp.clip(jnp.exp(math.log(0.2) - 2.3025851 * jax.random.uniform(arg_keys[5], (N_DP, DOCUMENT_LENGTH, TOP), jnp.float32) ** steps_of(arg_keys[5], (N_DP, DOCUMENT_LENGTH, TOP), ((0, 8), (1, 16)), -0.2, 0.2)), 0.02, 0.2),
        "trainable": draw_trainable(jax.random.fold_in(arg_keys[10], 71), 0),
        "norm_gain": jnp.clip(1.0 + 0.1 * jax.random.normal(arg_keys[7], (D,), jnp.float32), 0.5, 1.5),
        "upstream": gaussian(arg_keys[8], (N_DP, DOCUMENT_LENGTH, D), 1.0, 6.0, ((0, 8), (1, 16))),
        "expert_weights": gaussian(arg_keys[9], (TRAIN, H, 3, D), D ** -0.5, 0.09375, ((0, 16),)),
    }


MASK_FILLER = -1e+30
EPSILON = 1e-06

def positions(span_seq):
    row_index = jnp.arange(DOCUMENT_LENGTH, dtype=jnp.int32)
    half_rows = TOK_DEV // 2
    return span_seq[row_index // half_rows] * half_rows + row_index % half_rows

def head_scores(query_head, key_head, visible):
    raw_scores = jnp.dot(query_head, key_head.T, preferred_element_type=jnp.float32) * HEAD_SIZE ** (-0.5)
    return jnp.where(visible, raw_scores, MASK_FILLER)

def document_grads(query, key, value, span_seq, routes_now, gate_vals, trainable, norm_gain, upstream, expert_weights):
    heads_per_group = QUERY_HEADS // KEY_VALUE_HEADS
    place_now = positions(span_seq)
    visible = place_now[None, :] <= place_now[:, None]
    query_heads = query.reshape(DOCUMENT_LENGTH, QUERY_HEADS, HEAD_SIZE).transpose(1, 0, 2)
    key_head_rows = key.reshape(DOCUMENT_LENGTH, KEY_VALUE_HEADS, HEAD_SIZE).transpose(1, 0, 2)
    value_head_rows = value.reshape(DOCUMENT_LENGTH, KEY_VALUE_HEADS, HEAD_SIZE).transpose(1, 0, 2)
    head_number = jnp.arange(QUERY_HEADS, dtype=jnp.int32)

    def forward(item_now):
        query_head, number = item_now
        key_head = key_head_rows[number // heads_per_group]
        value_head = value_head_rows[number // heads_per_group]
        raw_scores = head_scores(query_head, key_head, visible)
        peak = lax.optimization_barrier(jnp.max(raw_scores, axis=1))
        spread = peak + jnp.log(lax.optimization_barrier(jnp.sum(jnp.exp(raw_scores - peak[:, None]), axis=1)))
        weights = jnp.where(visible, jnp.exp(raw_scores - spread[:, None]), 0.0).astype(jnp.bfloat16)
        output = jnp.dot(weights, value_head, preferred_element_type=jnp.float32).astype(jnp.bfloat16)
        return (output, spread)
    outputs, spreads = lax.map(forward, (query_heads, head_number))
    mixed_rows = outputs.transpose(1, 0, 2).reshape(DOCUMENT_LENGTH, D)
    features = mixed_rows.astype(jnp.float32)
    factor = lax.rsqrt(lax.optimization_barrier(jnp.mean(features * features, axis=1, keepdims=True)) + EPSILON)
    normed = (features * factor * norm_gain[None, :]).astype(jnp.bfloat16)
    most_rows = N_CTX * CAP

    def expert(item_now):
        expert_num, weights = item_now
        is_match = routes_now == expert_num
        chosen = jnp.any(is_match, axis=1)
        row_gate = lax.optimization_barrier(jnp.sum(jnp.where(is_match, gate_vals, 0.0), axis=1))
        picked = jnp.nonzero(chosen, size=most_rows, fill_value=0)[0].astype(jnp.int32)
        valid = jnp.arange(most_rows, dtype=jnp.int32) < jnp.sum(chosen.astype(jnp.int32))
        routed = jnp.where(valid[:, None], normed[picked], jnp.zeros((), jnp.bfloat16))
        weighted = jnp.where(valid[:, None], row_gate[picked][:, None] * upstream[picked].astype(jnp.float32), 0.0).astype(jnp.bfloat16)
        w_gate = weights[:, 0, :]
        w_up = weights[:, 1, :]
        w_down = weights[:, 2, :]
        gate_in = jnp.dot(routed, w_gate.T, preferred_element_type=jnp.float32)
        up_in = jnp.dot(routed, w_up.T, preferred_element_type=jnp.float32)
        back_grad = jnp.dot(weighted, w_down.T, preferred_element_type=jnp.float32)
        activated = jax.nn.silu(gate_in)
        product = (activated * up_in).astype(jnp.bfloat16)
        sigma = jax.nn.sigmoid(gate_in)
        grad_gate = (back_grad * up_in * sigma * (1.0 + gate_in * (1.0 - sigma))).astype(jnp.bfloat16)
        grad_up = (back_grad * activated).astype(jnp.bfloat16)
        returned = (jnp.dot(grad_gate, w_gate, preferred_element_type=jnp.float32) + jnp.dot(grad_up, w_up, preferred_element_type=jnp.float32)).astype(jnp.bfloat16)
        partial_sum = jnp.stack([jnp.dot(grad_gate.T, routed, preferred_element_type=jnp.float32), jnp.dot(grad_up.T, routed, preferred_element_type=jnp.float32), jnp.dot(product.T, weighted, preferred_element_type=jnp.float32)], axis=1)
        return (partial_sum, returned, picked, valid)
    partials, returned, picked, valid = lax.map(expert, (trainable, expert_weights))
    contrib = jnp.where(valid.reshape(-1)[:, None], returned.reshape(-1, D).astype(jnp.float32), 0.0)
    input_grad = jnp.zeros((DOCUMENT_LENGTH, D), jnp.float32).at[picked.reshape(-1)].add(contrib)
    gradnorm = norm_gain[None, :] * input_grad
    into_norm = factor * gradnorm - features * (factor * factor * factor) * lax.optimization_barrier(jnp.mean(gradnorm * features, axis=1, keepdims=True))
    grad_mixed = (upstream.astype(jnp.float32) + into_norm).astype(jnp.bfloat16)
    grad_heads = grad_mixed.reshape(DOCUMENT_LENGTH, QUERY_HEADS, HEAD_SIZE).transpose(1, 0, 2)

    def backward(item_now):
        query_head, out_head, grad_head, spread, number = item_now
        key_head = key_head_rows[number // heads_per_group]
        value_head = value_head_rows[number // heads_per_group]
        raw_scores = head_scores(query_head, key_head, visible)
        prob_full = jnp.where(visible, jnp.exp(raw_scores - spread[:, None]), 0.0)
        delta_sum = lax.optimization_barrier(jnp.sum(grad_head.astype(jnp.float32) * out_head.astype(jnp.float32), axis=1))
        pushed = jnp.dot(grad_head, value_head.T, preferred_element_type=jnp.float32)
        slopes = (prob_full * (pushed - delta_sum[:, None])).astype(jnp.bfloat16)
        inv_root = HEAD_SIZE ** (-0.5)
        query_grad = jnp.dot(slopes, key_head, preferred_element_type=jnp.float32) * inv_root
        key_grad = jnp.dot(slopes.T, query_head, preferred_element_type=jnp.float32) * inv_root
        value_grad = jnp.dot(prob_full.astype(jnp.bfloat16).T, grad_head, preferred_element_type=jnp.float32)
        return (query_grad, key_grad, value_grad)
    query_grads, key_gradient_list, value_gradient_list = lax.map(backward, (query_heads, outputs, grad_heads, spreads, head_number))
    d_query = query_grads.astype(jnp.bfloat16).transpose(1, 0, 2).reshape(DOCUMENT_LENGTH, QUERY_HEADS * HEAD_SIZE)
    key_gradient = lax.optimization_barrier(jnp.sum(key_gradient_list.reshape(KEY_VALUE_HEADS, heads_per_group, DOCUMENT_LENGTH, HEAD_SIZE), axis=1)).astype(jnp.bfloat16).transpose(1, 0, 2).reshape(DOCUMENT_LENGTH, KEY_VALUE_HEADS * HEAD_SIZE)
    value_gradient = lax.optimization_barrier(jnp.sum(value_gradient_list.reshape(KEY_VALUE_HEADS, heads_per_group, DOCUMENT_LENGTH, HEAD_SIZE), axis=1)).astype(jnp.bfloat16).transpose(1, 0, 2).reshape(DOCUMENT_LENGTH, KEY_VALUE_HEADS * HEAD_SIZE)
    return (d_query, key_gradient, value_gradient, partials)

def reference(query, key, value, span_order, expert_ids, expert_gates, trainable, norm_gain, upstream, expert_weights):
    query_list = []
    key_list = []
    value_list = []
    total_sum = jnp.zeros((TRAIN, H, 3, D), jnp.float32)
    for sequence in range(N_DP):
        d_query, key_gradient, value_gradient, partials = document_grads(query[sequence], key[sequence], value[sequence], span_order[sequence], expert_ids[sequence], expert_gates[sequence], trainable, norm_gain, upstream[sequence], expert_weights)
        query_list.append(d_query)
        key_list.append(key_gradient)
        value_list.append(value_gradient)
        total_sum = total_sum + lax.optimization_barrier(partials.astype(jnp.bfloat16)).astype(jnp.float32)
    return (jnp.stack(query_list), jnp.stack(key_list), jnp.stack(value_list), total_sum.astype(jnp.bfloat16))
```

```python
import jax
import jax.numpy as jnp
from jax import lax
from jax.sharding import PartitionSpec as P

D = 4096
QUERY_HEADS = 32
KEY_VALUE_HEADS = 2
HEAD_SIZE = 128
TOP = 8
CAP = 12


MASK_FILLER = -1e30
EPSILON = 1e-06


def sent_together(arrays, axis, dim, along):
    ends, at = ([], 0)
    for a in arrays[:-1]:
        at += a.shape[along]
        ends.append(at)
    both = jnp.concatenate(arrays, axis=along)
    return tuple(jnp.split(lax.all_gather(both, axis, axis=dim, tiled=True), ends, axis=along))


def side_by_side(arrays, axis, split_dim, concat_dim, along):
    both = jnp.concatenate(arrays, axis=along)
    filled, at, gathered = (
        lax.all_to_all(both, axis, split_axis=split_dim, concat_axis=concat_dim, tiled=True),
        0,
        [],
    )
    for a in arrays:
        gathered.append(lax.slice_in_dim(filled, at, at + a.shape[along], axis=along))
        at += a.shape[along]
    return tuple(gathered)


def in_blocks(array, dim, count):
    shape = array.shape
    tiles = array.reshape(*shape[:dim], count, shape[dim] // count, *shape[dim + 1 :])
    return jnp.moveaxis(tiles, dim, 0)


def sent_and_summed(array, axis, dim):
    count = lax.axis_size(axis)
    tiles = lax.all_to_all(in_blocks(array, dim, count), axis, 0, 0, tiled=True)
    return jnp.sum(tiles.astype(jnp.float32), axis=0)


def cross(left_arr, right_arr):
    return lax.dot_general(
        left_arr, right_arr, (((1,), (1,)), ((), ())), preferred_element_type=jnp.float32
    )


def inner(left_arr, right_arr):
    return lax.dot_general(
        left_arr, right_arr, (((0,), (0,)), ((), ())), preferred_element_type=jnp.float32
    )


def lookup(small_table, row_index):
    is_match = row_index[:, None] == jnp.arange(small_table.shape[0], dtype=jnp.int32)[None, :]
    return jnp.sum(jnp.where(is_match, small_table[None, :], 0), axis=1)


def blockwise(stepper, initial, wholes):
    total_rows = wholes[0].shape[0]
    block_rows = min(512, total_rows)

    def step_num(number, running):
        begin_at = number * block_rows
        segment_list = tuple(
            (lax.dynamic_slice_in_dim(whole, begin_at, block_rows, 0) for whole in wholes)
        )
        return stepper(running, segment_list, begin_at)

    return lax.fori_loop(0, total_rows // block_rows, step_num, initial)


def expert_terms_of(grad_gate, grad_up, product, routed, weighted):
    return jnp.stack(
        [inner(grad_gate, routed), inner(grad_up, routed), inner(product, weighted)], axis=1
    )


def per_device(
    query,
    key,
    value,
    span_order,
    expert_ids,
    expert_gates,
    trainable,
    norm_gain,
    upstream,
    expert_weights,
):
    token_rows = query.shape[1]
    half_rows = token_rows // 2
    heads_per_group = QUERY_HEADS // KEY_VALUE_HEADS
    inv_root = HEAD_SIZE ** (-0.5)
    span_seq = span_order[0]
    ctx_count = lax.axis_size("ctx")
    first_row = lax.axis_index("ctx") * token_rows

    def place(begin_at, total_count):
        row_index = begin_at + jnp.arange(total_count, dtype=jnp.int32)
        return lookup(span_seq, row_index // half_rows) * half_rows + row_index % half_rows

    query_place = place(first_row, token_rows)
    query_rows = jnp.tile(query_place, heads_per_group)

    def by_head(flattened_rows):
        return (
            flattened_rows.reshape(token_rows, KEY_VALUE_HEADS, heads_per_group, HEAD_SIZE)
            .transpose(1, 2, 0, 3)
            .reshape(KEY_VALUE_HEADS, heads_per_group * token_rows, HEAD_SIZE)
        )

    def by_row(stacked_rows):
        return (
            stacked_rows.reshape(KEY_VALUE_HEADS, heads_per_group, token_rows, HEAD_SIZE)
            .transpose(2, 0, 1, 3)
            .reshape(token_rows, QUERY_HEADS * HEAD_SIZE)
        )

    queries = by_head(query[0])
    query_count = heads_per_group * token_rows

    def scores(key_row_block, begin_at):
        total_count = key_row_block.shape[0]
        visible = (place(begin_at, total_count)[None, :] <= query_rows[:, None])[None, :, :]
        raw_scores = (
            jnp.einsum(
                "gqd,kgd->gqk",
                queries,
                key_row_block.reshape(total_count, KEY_VALUE_HEADS, HEAD_SIZE),
                preferred_element_type=jnp.float32,
            )
            * inv_root
        )
        return (jnp.where(visible, raw_scores, MASK_FILLER), visible)

    def guarded(stepper):

        def run_step(running, segment_list, begin_at):
            return stepper(running, segment_list, begin_at)

        return run_step

    def stats_step(running, segment_list, begin_at):
        largest_score, total_sum = running
        raw_scores, visible = scores(segment_list[0], begin_at)
        newest = jnp.maximum(largest_score, jnp.max(raw_scores, axis=2))
        exps = jnp.where(visible, jnp.exp(raw_scores - newest[:, :, None]), 0.0)
        return (newest, total_sum * jnp.exp(largest_score - newest) + jnp.sum(exps, axis=2))

    stats_init = (
        jnp.full((KEY_VALUE_HEADS, query_count), MASK_FILLER, jnp.float32),
        jnp.zeros((KEY_VALUE_HEADS, query_count), jnp.float32),
    )
    whole_keys, whole_values = sent_together((key[0], value[0]), "ctx", 0, 1)
    largest_score, total_sum = blockwise(guarded(stats_step), stats_init, (whole_keys,))
    spread = largest_score + jnp.log(total_sum)

    def output_step(running, segment_list, begin_at):
        raw_scores, visible = scores(segment_list[0], begin_at)
        weights = jnp.where(visible, jnp.exp(raw_scores - spread[:, :, None]), 0.0).astype(
            jnp.bfloat16
        )
        present_values = segment_list[1].reshape(-1, KEY_VALUE_HEADS, HEAD_SIZE)
        return running + jnp.einsum(
            "gqk,kgd->gqd", weights, present_values, preferred_element_type=jnp.float32
        )

    out_init = jnp.zeros((KEY_VALUE_HEADS, query_count, HEAD_SIZE), jnp.float32)
    attended = blockwise(guarded(output_step), out_init, (whole_keys, whole_values))
    heads_out = attended.astype(jnp.bfloat16)
    mixed_rows = by_row(heads_out)
    features = mixed_rows.astype(jnp.float32)
    factor = lax.rsqrt(jnp.mean(features * features, axis=1, keepdims=True) + EPSILON)
    normed = (features * factor * norm_gain[None, :]).astype(jnp.bfloat16)
    routes_now = expert_ids[0]
    gate_vals = expert_gates[0]
    grad_out = upstream[0]
    slot_count = trainable.shape[0]
    is_match = (routes_now[:, :, None] == trainable[None, None, :]).astype(jnp.int32)
    flat_hits = is_match.reshape(token_rows * TOP, slot_count)
    flat_index = jnp.arange(token_rows * TOP, dtype=jnp.int32)
    earlier = (flat_index[None, :] < flat_index[:, None]).astype(jnp.bfloat16)
    slot_rank = jnp.dot(
        earlier, flat_hits.astype(jnp.bfloat16), preferred_element_type=jnp.float32
    ).astype(jnp.int32)
    chosen = (flat_hits[:, :, None] == 1) & (
        slot_rank[:, :, None] == jnp.arange(CAP, dtype=jnp.int32)[None, None, :]
    )
    chosen = chosen.reshape(token_rows, TOP, slot_count * CAP)
    pick_mask = jnp.sum(chosen.astype(jnp.float32), axis=1).astype(jnp.bfloat16)
    slot_gate = jnp.sum(jnp.where(chosen, gate_vals[:, :, None], 0.0), axis=(0, 1))
    sent_rows = inner(pick_mask, normed).astype(jnp.bfloat16)
    sent_grads = (slot_gate[:, None] * inner(pick_mask, grad_out)).astype(jnp.bfloat16)
    arrived_rows, arrived_grads = side_by_side(
        (sent_rows.reshape(slot_count, CAP, D), sent_grads.reshape(slot_count, CAP, D)),
        "ctx",
        0,
        0,
        1,
    )
    routed = arrived_rows.reshape(-1, D)
    weighted = arrived_grads.reshape(-1, D)
    weights_all = expert_weights[0]
    w_gate = weights_all[:, 0, :]
    w_up = weights_all[:, 1, :]
    w_down = weights_all[:, 2, :]
    gate_in = cross(routed, w_gate)
    up_in = cross(routed, w_up)
    back_grad = cross(weighted, w_down)
    activated = jax.nn.silu(gate_in)
    product = (activated * up_in).astype(jnp.bfloat16)
    sigma = jax.nn.sigmoid(gate_in)
    grad_gate = (back_grad * up_in * sigma * (1.0 + gate_in * (1.0 - sigma))).astype(jnp.bfloat16)
    grad_up = (back_grad * activated).astype(jnp.bfloat16)
    returned = (
        jnp.dot(grad_gate, w_gate, preferred_element_type=jnp.float32)
        + jnp.dot(grad_up, w_up, preferred_element_type=jnp.float32)
    ).astype(jnp.bfloat16)
    echoed = lax.all_to_all(
        returned.reshape(-1, CAP, D), "ctx", split_axis=0, concat_axis=0, tiled=True
    )
    input_grad = jnp.dot(
        pick_mask, echoed.reshape(slot_count * CAP, D), preferred_element_type=jnp.float32
    )
    summed = lax.psum_scatter(
        expert_terms_of(grad_gate, grad_up, product, routed, weighted).astype(jnp.bfloat16),
        "dp",
        scatter_dimension=0,
        tiled=True,
    )
    expert_grads = summed[None]
    gradnorm = norm_gain[None, :] * input_grad
    into_norm = factor * gradnorm - features * (factor * factor * factor) * jnp.mean(
        gradnorm * features, axis=1, keepdims=True
    )
    grad_mixed = (grad_out.astype(jnp.float32) + into_norm).astype(jnp.bfloat16)
    grad_heads = by_head(grad_mixed)
    delta_sum = jnp.sum(grad_heads.astype(jnp.float32) * heads_out.astype(jnp.float32), axis=2)

    def grad_step(running, segment_list, begin_at):
        query_grad, key_grad = running
        total_count = segment_list[0].shape[0]
        raw_scores, visible = scores(segment_list[0], begin_at)
        prob_full = jnp.where(visible, jnp.exp(raw_scores - spread[:, :, None]), 0.0)
        present_keys = segment_list[0].reshape(total_count, KEY_VALUE_HEADS, HEAD_SIZE)
        present_values = segment_list[1].reshape(total_count, KEY_VALUE_HEADS, HEAD_SIZE)
        pushed = jnp.einsum(
            "gqd,kgd->gqk", grad_heads, present_values, preferred_element_type=jnp.float32
        )
        slopes = (prob_full * (pushed - delta_sum[:, :, None])).astype(jnp.bfloat16)
        query_grad = (
            query_grad
            + jnp.einsum("gqk,kgd->gqd", slopes, present_keys, preferred_element_type=jnp.float32)
            * inv_root
        )
        key_portion = (
            jnp.einsum("gqk,gqd->kgd", slopes, queries, preferred_element_type=jnp.float32)
            * inv_root
        )
        value_portion = jnp.einsum(
            "gqk,gqd->kgd",
            prob_full.astype(jnp.bfloat16),
            grad_heads,
            preferred_element_type=jnp.float32,
        )
        update = jnp.concatenate(
            [
                key_portion.reshape(total_count, KEY_VALUE_HEADS * HEAD_SIZE),
                value_portion.reshape(total_count, KEY_VALUE_HEADS * HEAD_SIZE),
            ],
            axis=1,
        )
        current = lax.dynamic_slice_in_dim(key_grad, begin_at, total_count, 0)
        return (
            query_grad,
            lax.dynamic_update_slice_in_dim(key_grad, current + update, begin_at, 0),
        )

    grad_init = (
        jnp.zeros((KEY_VALUE_HEADS, query_count, HEAD_SIZE), jnp.float32),
        jnp.zeros((token_rows * ctx_count, 2 * KEY_VALUE_HEADS * HEAD_SIZE), jnp.float32),
    )
    query_grad, key_grad = blockwise(guarded(grad_step), grad_init, (whole_keys, whole_values))
    key_sum_totals = sent_and_summed(key_grad.astype(jnp.bfloat16), "ctx", 0)
    d_query = by_row(query_grad.astype(jnp.bfloat16))[None]
    key_gradient = key_sum_totals[:, : KEY_VALUE_HEADS * HEAD_SIZE].astype(jnp.bfloat16)[None]
    value_gradient = key_sum_totals[:, KEY_VALUE_HEADS * HEAD_SIZE :].astype(jnp.bfloat16)[None]
    return (d_query, key_gradient, value_gradient, expert_grads)


def solution(mesh):
    in_specs = (
        P("dp", "ctx", None),
        P("dp", "ctx", None),
        P("dp", "ctx", None),
        P("dp", None),
        P("dp", "ctx", None),
        P("dp", "ctx", None),
        P(),
        P(),
        P("dp", "ctx", None),
        P("ctx", None, None, None),
    )
    out_specs = (
        P("dp", "ctx", None),
        P("dp", "ctx", None),
        P("dp", "ctx", None),
        P("ctx", "dp", None, None),
    )
    return jax.shard_map(
        per_device, mesh=mesh, in_specs=in_specs, out_specs=out_specs, check_vma=False
    )
```

```python
import math

import jax
import jax.numpy as jnp
from jax import lax
from jax.experimental import pallas as pl
from jax.experimental.pallas import tpu as pltpu
from jax.sharding import PartitionSpec as P

D = 4096
QUERY_HEADS = 32
KEY_VALUE_HEADS = 2
HEAD_SIZE = 128
TOP = 8
CAP = 12
H = 768
N_CTX = 16
N_CHIP = 8
ROWS = 128
KEYS = 2048
SLOTS = 16
FOLDS = 4
WIDE = D // FOLDS
SLAB = CAP * FOLDS
SLAB_ROWS = SLOTS * SLAB
PAIRS = QUERY_HEADS // 2
KEY_BLOCK = 512

MASK_FILLER = -1e30
EPSILON = 1e-06
INV_ROOT = HEAD_SIZE ** (-0.5)
TO_BASE_TWO = INV_ROOT * math.log2(math.e)

MESH = pl.DeviceIdType.MESH
VMEM_LIMIT = 60 * 2**20
BF = jnp.bfloat16
F32 = jnp.float32


def dot_nn(a, b):
    return lax.dot_general(a, b, (((1,), (0,)), ((), ())), preferred_element_type=F32)


def dot_nt(a, b):
    return lax.dot_general(a, b, (((1,), (1,)), ((), ())), preferred_element_type=F32)


def dot_tn(a, b):
    return lax.dot_general(a, b, (((0,), (0,)), ((), ())), preferred_element_type=F32)


def in_vmem(count):
    return [pl.BlockSpec(memory_space=pltpu.VMEM)] * count


def local(cost):
    return dict(
        compiler_params=pltpu.CompilerParams(vmem_limit_bytes=VMEM_LIMIT),
        cost_estimate=pl.CostEstimate(flops=cost, bytes_accessed=2**22, transcendentals=0),
    )


def slot_masks(ids_ref, gates_ref, trainable_ref):
    experts = trainable_ref[...]
    hits = jnp.zeros((SLOTS, ROWS), F32)
    gates = jnp.zeros((SLOTS, ROWS), F32)
    for k in range(TOP):
        same = ids_ref[k : k + 1, :] == experts
        hits = hits + jnp.where(same, 1.0, 0.0)
        gates = gates + jnp.where(same, gates_ref[k : k + 1, :], 0.0)
    before = lax.broadcasted_iota(jnp.int32, (ROWS, ROWS), 0) < lax.broadcasted_iota(
        jnp.int32, (ROWS, ROWS), 1
    )
    rank = dot_nn(hits.astype(BF), jnp.where(before, 1.0, 0.0).astype(BF))
    rank = jnp.where(hits > 0.5, rank, -1.0)
    row = lax.broadcasted_iota(jnp.int32, (SLAB, 1), 0)
    fold = sum(jnp.where(row >= CAP * f, 1, 0) for f in range(1, FOLDS))
    within = (row - CAP * fold).astype(F32)
    masks = [[] for _ in range(FOLDS)]
    row_gate = []
    for j in range(SLOTS):
        match = jnp.broadcast_to(rank[j : j + 1, :], (SLAB, ROWS)) == within
        row_gate.append(
            jnp.sum(jnp.where(match, gates[j : j + 1, :], 0.0), axis=1, keepdims=True)
        )
        for f in range(FOLDS):
            masks[f].append(jnp.where(match & (fold == f), 1.0, 0.0))
    return (
        [jnp.concatenate(m, axis=0).astype(BF) for m in masks],
        jnp.concatenate(row_gate, axis=0),
    )


def fold_of(ref, f):
    return ref[:, f * WIDE : (f + 1) * WIDE]


def unfold_mask(f):
    n = lax.broadcasted_iota(jnp.int32, (SLOTS * CAP, SLAB_ROWS), 0)
    m = lax.broadcasted_iota(jnp.int32, (SLOTS * CAP, SLAB_ROWS), 1)
    source = lax.shift_right_logical(n * 5462, 16)
    return jnp.where(m == n + (SLAB - CAP) * source + CAP * f, 1.0, 0.0).astype(BF)


def refold_mask(f):
    n = lax.broadcasted_iota(jnp.int32, (SLAB_ROWS, SLOTS * CAP), 1)
    m = lax.broadcasted_iota(jnp.int32, (SLAB_ROWS, SLOTS * CAP), 0)
    source = lax.shift_right_logical(n * 5462, 16)
    return jnp.where(m == n + (SLAB - CAP) * source + CAP * f, 1.0, 0.0).astype(BF)


def weighted_kernel(ids_ref, gates_ref, trainable_ref, up_ref, out_ref):
    masks, row_gate = slot_masks(ids_ref, gates_ref, trainable_ref)
    total = dot_nn(masks[0], fold_of(up_ref, 0))
    for f in range(1, FOLDS):
        total = total + dot_nn(masks[f], fold_of(up_ref, f))
    out_ref[...] = (row_gate * total).astype(BF)


def two_heads(ref, pair):
    at = pl.multiple_of(pair * 2 * HEAD_SIZE, 2 * HEAD_SIZE)
    both = ref[:, pl.ds(at, 2 * HEAD_SIZE)]
    return jnp.concatenate([both[:, :HEAD_SIZE], both[:, HEAD_SIZE:]], axis=0)


def put_two_heads(ref, pair, stacked):
    at = pl.multiple_of(pair * 2 * HEAD_SIZE, 2 * HEAD_SIZE)
    ref[:, pl.ds(at, 2 * HEAD_SIZE)] = jnp.concatenate([stacked[:ROWS], stacked[ROWS:]], axis=1)


def diagonal():
    eye = lax.broadcasted_iota(jnp.int32, (ROWS, ROWS), 0) == lax.broadcasted_iota(
        jnp.int32, (ROWS, ROWS), 1
    )
    one = jnp.where(eye, MASK_FILLER, 0.0).astype(BF)
    return jnp.concatenate([one, one], axis=0)


def rms_factor(features):
    return lax.rsqrt(jnp.mean(features * features, axis=1, keepdims=True) + EPSILON)


def forward_kernel(
    q_ref, kv_ref, hidden_ref, ids_ref, gates_ref, trainable_ref, gain_ref,
    mixed_ref, spread_ref, slab_ref,
    masked_keys, values_t, hides, scores,
):
    for g in range(KEY_VALUE_HEADS):
        masked_keys[g, :, :HEAD_SIZE] = kv_ref[:, g * HEAD_SIZE : (g + 1) * HEAD_SIZE]
        masked_keys[g, :, HEAD_SIZE:] = hidden_ref[...]
        at = (KEY_VALUE_HEADS + g) * HEAD_SIZE
        values_t[g] = kv_ref[:, at : at + HEAD_SIZE].T
    hides[...] = diagonal()

    def step(pair, carry):
        g = lax.div(pair, PAIRS // KEY_VALUE_HEADS)
        queries = jnp.concatenate([two_heads(q_ref, pair), hides[...]], axis=1)
        peak = None
        for b in range(KEYS // KEY_BLOCK):
            rows = slice(b * KEY_BLOCK, (b + 1) * KEY_BLOCK)
            block = dot_nt(masked_keys[g, rows, :], queries)
            scores[rows, :] = block
            top = jnp.max(block, axis=0, keepdims=True)
            peak = top if peak is None else jnp.maximum(peak, top)
        total, out = None, None
        for b in range(KEYS // KEY_BLOCK):
            rows = slice(b * KEY_BLOCK, (b + 1) * KEY_BLOCK)
            exps = jnp.exp2((scores[rows, :] - peak) * TO_BASE_TWO)
            part = jnp.sum(exps, axis=0, keepdims=True)
            piece = dot_nn(values_t[g, :, rows], exps.astype(BF))
            total = part if total is None else total + part
            out = piece if out is None else out + piece
        put_two_heads(mixed_ref, pair, (out / total).T.astype(BF))
        spread_ref[pl.ds(pair, 1), :] = peak * TO_BASE_TWO + jnp.log2(total)
        return carry

    lax.fori_loop(0, PAIRS, step, 0)
    features = mixed_ref[...].astype(F32)
    normed = (features * rms_factor(features) * gain_ref[...]).astype(BF)
    masks, _ = slot_masks(ids_ref, gates_ref, trainable_ref)
    picked = dot_nn(masks[0], fold_of(normed, 0))
    for f in range(1, FOLDS):
        picked = picked + dot_nn(masks[f], fold_of(normed, f))
    slab_ref[...] = picked.astype(BF)


def expert_kernel(rows_ref, grads_ref, w_ref, terms_ref, back_ref, routed, weighted, returned):
    step = pl.program_id(0)

    @pl.when(step == 0)
    def _():
        for f in range(FOLDS):
            pick = unfold_mask(f)
            routed[:, f * WIDE : (f + 1) * WIDE] = dot_nn(pick, rows_ref[...]).astype(BF)
            weighted[:, f * WIDE : (f + 1) * WIDE] = dot_nn(pick, grads_ref[...]).astype(BF)

    gate_in = dot_nt(routed[...], w_ref[0])
    up_in = dot_nt(routed[...], w_ref[1])
    back = dot_nt(weighted[...], w_ref[2])
    sigma = jax.nn.sigmoid(gate_in)
    activated = gate_in * sigma
    grad_gate = (back * up_in * sigma * (1.0 + gate_in * (1.0 - sigma))).astype(BF)
    grad_up = (back * activated).astype(BF)
    terms_ref[0] = grad_gate
    terms_ref[1] = grad_up
    terms_ref[2] = (activated * up_in).astype(BF)
    for f in range(FOLDS):
        at = slice(f * WIDE, (f + 1) * WIDE)
        part = dot_nn(grad_gate, w_ref[0, :, at]) + dot_nn(grad_up, w_ref[1, :, at])

        @pl.when(step == 0)
        def _():
            returned[:, at] = part

        @pl.when(step > 0)
        def _():
            returned[:, at] += part

    @pl.when(step == pl.num_programs(0) - 1)
    def _():
        total = dot_nn(refold_mask(0), returned[:, :WIDE].astype(BF))
        for f in range(1, FOLDS):
            at = slice(f * WIDE, (f + 1) * WIDE)
            total = total + dot_nn(refold_mask(f), returned[:, at].astype(BF))
        back_ref[...] = total.astype(BF)


def terms_kernel(own_ref, other_ref, own_terms_ref, other_terms_ref, out_ref):
    for f in range(FOLDS):
        pick = unfold_mask(f)
        own = dot_nn(pick, own_ref[...]).astype(BF)
        other = dot_nn(pick, other_ref[...]).astype(BF)
        for i in range(out_ref.shape[0]):
            out_ref[i, :, f * WIDE : (f + 1) * WIDE] = (
                dot_tn(own_terms_ref[i], own) + dot_tn(other_terms_ref[i], other)
            ).astype(BF)


def backward_kernel(
    q_ref, kv_ref, hidden_ref, ids_ref, gates_ref, trainable_ref, gain_ref,
    mixed_ref, spread_ref, up_ref, echo_ref,
    d_query_ref, d_kv_ref,
    masked_keys, keys_t, hides, grad_mixed, key_sums, value_sums,
):
    for g in range(KEY_VALUE_HEADS):
        keys = kv_ref[:, g * HEAD_SIZE : (g + 1) * HEAD_SIZE]
        masked_keys[g, :, :HEAD_SIZE] = keys
        masked_keys[g, :, HEAD_SIZE:] = hidden_ref[...]
        keys_t[g] = keys.T
    hides[...] = diagonal()
    key_sums[...] = jnp.zeros_like(key_sums)
    value_sums[...] = jnp.zeros_like(value_sums)

    masks, _ = slot_masks(ids_ref, gates_ref, trainable_ref)
    features = mixed_ref[...].astype(F32)
    factor = rms_factor(features)
    gradnorm = gain_ref[...] * jnp.concatenate(
        [dot_tn(m, echo_ref[...]) for m in masks], axis=1
    )
    across = jnp.mean(gradnorm * features, axis=1, keepdims=True)
    grad_mixed[...] = (
        up_ref[...].astype(F32)
        + factor * gradnorm
        - features * (factor * factor * factor) * across
    ).astype(BF)

    def step(pair, carry):
        g = lax.div(pair, PAIRS // KEY_VALUE_HEADS)
        plain = two_heads(q_ref, pair)
        queries = jnp.concatenate([plain, hides[...]], axis=1)
        grads = two_heads(grad_mixed, pair)
        products = grads.astype(F32) * two_heads(mixed_ref, pair).astype(F32)
        delta = jnp.sum(products.T, axis=0, keepdims=True)
        spread = spread_ref[pl.ds(pair, 1), :]
        d_query = None
        for b in range(KEYS // KEY_BLOCK):
            rows = slice(b * KEY_BLOCK, (b + 1) * KEY_BLOCK)
            at = (KEY_VALUE_HEADS + g) * HEAD_SIZE
            values = kv_ref[rows, pl.ds(pl.multiple_of(at, HEAD_SIZE), HEAD_SIZE)]
            raw = dot_nt(masked_keys[g, rows, :], queries)
            probs = jnp.exp2(raw * TO_BASE_TWO - spread)
            pushed = dot_nt(values, grads)
            slopes = (probs * (pushed - delta)).astype(BF)
            value_sums[g, rows, :] += dot_nn(probs.astype(BF), grads)
            key_sums[g, rows, :] += dot_nn(slopes, plain)
            piece = dot_nn(keys_t[g, :, rows], slopes)
            d_query = piece if d_query is None else d_query + piece
        put_two_heads(d_query_ref, pair, (d_query * INV_ROOT).T.astype(BF))
        return carry

    lax.fori_loop(0, PAIRS, step, 0)
    for g in range(KEY_VALUE_HEADS):
        at = g * HEAD_SIZE
        d_kv_ref[:, at : at + HEAD_SIZE] = (key_sums[g] * INV_ROOT).astype(BF)
        at = (KEY_VALUE_HEADS + g) * HEAD_SIZE
        d_kv_ref[:, at : at + HEAD_SIZE] = value_sums[g].astype(BF)


def greet(targets):
    barrier = pltpu.get_barrier_semaphore()
    for target in targets:
        pl.semaphore_signal(barrier, inc=1, device_id={"ctx": target}, device_id_type=MESH)
    pl.semaphore_wait(barrier, len(targets))


def send(source, target, send_sem, recv_sem, device):
    return pltpu.make_async_remote_copy(
        src_ref=source, dst_ref=target, send_sem=send_sem, recv_sem=recv_sem,
        device_id={"ctx": device}, device_id_type=MESH,
    )


def exchange_kernel(x_ref, out_ref, send_sem, recv_sem, own_sem):
    me = lax.axis_index("ctx")
    others = [lax.rem(me + d, N_CTX) for d in range(1, N_CTX)]
    greet(others)
    copies = []
    for d, other in enumerate(others):
        copy = send(x_ref.at[other], out_ref.at[me], send_sem.at[d], recv_sem.at[d], other)
        copy.start()
        copies.append(copy)
    own = pltpu.make_async_copy(x_ref.at[me], out_ref.at[me], own_sem)
    own.start()
    for copy in copies:
        copy.wait()
    own.wait()


def gather_kernel(x_ref, out_ref, send_sem, recv_sem, pass_sem, passed_sem, near_sem, own_sem):
    me = lax.axis_index("ctx")
    chip, core = lax.div(me, 2), lax.rem(me, 2)
    sibling = 2 * chip + 1 - core
    far = [2 * lax.rem(chip + d, N_CHIP) + core for d in range(1, N_CHIP)]
    greet([*far, sibling])
    copies = []
    for d, other in enumerate(far):
        copy = send(x_ref, out_ref.at[me], send_sem.at[d], recv_sem.at[d], other)
        copy.start()
        copies.append(copy)
    near = send(x_ref, out_ref.at[me], near_sem.at[0], near_sem.at[1], sibling)
    near.start()
    own = pltpu.make_async_copy(x_ref, out_ref.at[me], own_sem)
    own.start()
    passed = []
    for d in range(1, N_CHIP):
        source = 2 * lax.rem(chip + N_CHIP - d, N_CHIP) + core
        copies[d - 1].wait_recv()
        copy = send(
            out_ref.at[source], out_ref.at[source],
            pass_sem.at[d - 1], passed_sem.at[d - 1], sibling,
        )
        copy.start()
        passed.append(copy)
    for copy in copies:
        copy.wait_send()
    near.wait()
    own.wait()
    for copy in passed:
        copy.wait()


def scatter_kernel(
    x_ref, out_ref, near, sums, landed, near_send, near_recv, send_sem, recv_sem
):
    me = lax.axis_index("ctx")
    chip, core = lax.div(me, 2), lax.rem(me, 2)
    sibling = 2 * chip + 1 - core
    chips = [lax.rem(chip + d, N_CHIP) for d in range(N_CHIP)]
    greet([*(2 * c + core for c in chips[1:]), sibling])
    order = [*range(1, N_CHIP), 0]
    shared = {}
    for d in order:
        copy = send(
            x_ref.at[2 * chips[d] + 1 - core], near.at[d], near_send.at[d], near_recv.at[d], sibling
        )
        copy.start()
        shared[d] = copy
    copies = []
    for d in order:
        shared[d].wait_recv()
        both = x_ref[2 * chips[d] + core].astype(F32) + near[d].astype(F32)
        if d == 0:
            total = both
        else:
            sums[d] = both.astype(BF)
            copy = send(
                sums.at[d], landed.at[d], send_sem.at[d], recv_sem.at[d], 2 * chips[d] + core
            )
            copy.start()
            copies.append(copy)
    for d, copy in enumerate(copies, start=1):
        copy.wait_recv()
        total = total + landed[d].astype(F32)
    out_ref[...] = total.astype(BF)
    for copy in copies:
        copy.wait_send()
    for d in order:
        shared[d].wait_send()


def dma(count):
    return pltpu.SemaphoreType.DMA((count,))


def remote(kernel, shape, scratch, number, sent):
    return pl.pallas_call(
        kernel,
        out_shape=jax.ShapeDtypeStruct(shape, BF),
        in_specs=in_vmem(1),
        out_specs=in_vmem(1)[0],
        scratch_shapes=scratch,
        compiler_params=pltpu.CompilerParams(
            collective_id=number, has_side_effects=True, vmem_limit_bytes=VMEM_LIMIT
        ),
        cost_estimate=pl.CostEstimate(flops=0, bytes_accessed=sent, transcendentals=0),
    )


def exchange(slabs, number):
    shape = (SLOTS, SLAB, WIDE)
    scratch = [dma(N_CTX - 1), dma(N_CTX - 1), pltpu.SemaphoreType.DMA]
    out = remote(exchange_kernel, shape, scratch, number, 2**26)(slabs.reshape(shape))
    return out.reshape(SLAB_ROWS, WIDE)


def gather(block):
    scratch = [dma(7), dma(7), dma(7), dma(7), dma(2), pltpu.SemaphoreType.DMA]
    out = remote(gather_kernel, (N_CTX, *block.shape), scratch, 0, 2**26)(block)
    return out.reshape(-1, block.shape[1])


def scatter_sum(parts):
    blocks = parts.reshape(N_CTX, ROWS, -1)
    block = blocks.shape[1:]
    slots = pltpu.VMEM((N_CHIP, *block), BF)
    scratch = [slots, slots, slots, dma(8), dma(8), dma(8), dma(8)]
    return remote(scatter_kernel, block, scratch, 3, 2**26)(blocks)


def over_pair(array):
    return lax.ppermute(array, "dp", [(i, (i + 4) % 8) for i in range(8)])


def summed_over_x(array):
    return lax.psum_scatter(
        array, "dp", scatter_dimension=1, tiled=True,
        axis_index_groups=[[0, 1, 2, 3], [4, 5, 6, 7]],
    )


def per_device(
    query, key, value, span_order, expert_ids, expert_gates,
    trainable, norm_gain, upstream, expert_weights,
):
    bf_shape = lambda *s: jax.ShapeDtypeStruct(s, BF)
    half = ROWS // 2
    place = (span_order[0][:, None] * half + jnp.arange(half, dtype=jnp.int32)[None, :]).reshape(-1)
    own_place = lax.dynamic_slice_in_dim(place, lax.axis_index("ctx") * ROWS, ROWS)
    hidden = (place[:, None] > own_place[None, :]).astype(BF)
    tables = (expert_ids[0].T, expert_gates[0].T, trainable[:, None])
    gain = norm_gain[None, :]
    weights = expert_weights[0].transpose(1, 0, 2)

    slab_shape = bf_shape(SLAB_ROWS, WIDE)
    sent_grads = pl.pallas_call(
        weighted_kernel, out_shape=slab_shape, in_specs=in_vmem(4), out_specs=in_vmem(1)[0],
        name="weighted", **local(10**9),
    )(*tables, upstream[0])
    grads = lax.all_to_all(
        sent_grads.reshape(SLOTS, SLAB, WIDE), "ctx", split_axis=0, concat_axis=0, tiled=True
    ).reshape(SLAB_ROWS, WIDE)
    other_grads = over_pair(grads)

    whole = gather(jnp.concatenate([key[0], value[0]], axis=1))
    groups = KEY_VALUE_HEADS
    mixed, spread, sent_rows = pl.pallas_call(
        forward_kernel,
        out_shape=(
            bf_shape(ROWS, D),
            jax.ShapeDtypeStruct((PAIRS, 2 * ROWS), F32),
            slab_shape,
        ),
        in_specs=in_vmem(7),
        out_specs=tuple(in_vmem(3)),
        scratch_shapes=[
            pltpu.VMEM((groups, KEYS, 2 * HEAD_SIZE), BF),
            pltpu.VMEM((groups, HEAD_SIZE, KEYS), BF),
            pltpu.VMEM((2 * ROWS, ROWS), BF),
            pltpu.VMEM((KEYS, 2 * ROWS), F32),
        ],
        name="attention",
        **local(2 * 10**10),
    )(query[0], whole, hidden, *tables, gain)

    rows = exchange(sent_rows, 1)
    other_rows = over_pair(rows)

    block = 256
    terms, sent_back = pl.pallas_call(
        expert_kernel,
        grid=(H // block,),
        out_shape=(bf_shape(3, SLOTS * CAP, H), slab_shape),
        in_specs=[
            pl.BlockSpec((SLAB_ROWS, WIDE), lambda i: (0, 0)),
            pl.BlockSpec((SLAB_ROWS, WIDE), lambda i: (0, 0)),
            pl.BlockSpec((3, block, D), lambda i: (0, i, 0)),
        ],
        out_specs=(
            pl.BlockSpec((3, SLOTS * CAP, block), lambda i: (0, 0, i)),
            pl.BlockSpec((SLAB_ROWS, WIDE), lambda i: (0, 0)),
        ),
        scratch_shapes=[
            pltpu.VMEM((SLOTS * CAP, D), BF),
            pltpu.VMEM((SLOTS * CAP, D), BF),
            pltpu.VMEM((SLOTS * CAP, D), F32),
        ],
        name="experts",
        **local(10**10),
    )(rows, grads, weights)

    mine = lax.div(lax.axis_index("dp"), 4)
    kept = lax.dynamic_slice_in_dim(terms, mine * (H // 2), H // 2, 2)
    given = lax.dynamic_slice_in_dim(terms, (1 - mine) * (H // 2), H // 2, 2)
    taken = over_pair(given)

    def partial(own, other, at, count, name):
        return pl.pallas_call(
            terms_kernel, out_shape=bf_shape(count, H // 2, D),
            in_specs=in_vmem(4), out_specs=in_vmem(1)[0], name=name, **local(4 * 10**9),
        )(own, other, kept[at : at + count], taken[at : at + count])

    down = summed_over_x(partial(grads, other_grads, 2, 1, "down_terms"))
    echo = exchange(sent_back, 2)
    gate_up = summed_over_x(partial(rows, other_rows, 0, 2, "gate_up_terms"))

    d_query, d_kv = pl.pallas_call(
        backward_kernel,
        out_shape=(bf_shape(ROWS, D), bf_shape(KEYS, 2 * groups * HEAD_SIZE)),
        in_specs=in_vmem(11),
        out_specs=tuple(in_vmem(2)),
        scratch_shapes=[
            pltpu.VMEM((groups, KEYS, 2 * HEAD_SIZE), BF),
            pltpu.VMEM((groups, HEAD_SIZE, KEYS), BF),
            pltpu.VMEM((2 * ROWS, ROWS), BF),
            pltpu.VMEM((ROWS, D), BF),
            pltpu.VMEM((groups, KEYS, HEAD_SIZE), F32),
            pltpu.VMEM((groups, KEYS, HEAD_SIZE), F32),
        ],
        name="attention_grads",
        **local(4 * 10**10),
    )(query[0], whole, hidden, *tables, gain, mixed, spread, upstream[0], echo)
    kv_sums = scatter_sum(d_kv)
    split = groups * HEAD_SIZE
    expert_grads = jnp.concatenate([gate_up, down], axis=0).transpose(1, 0, 2)
    return (
        d_query[None],
        kv_sums[None, :, :split],
        kv_sums[None, :, split:],
        expert_grads[None],
    )


def solution(mesh):
    in_specs = (
        P("dp", "ctx", None),
        P("dp", "ctx", None),
        P("dp", "ctx", None),
        P("dp", None),
        P("dp", "ctx", None),
        P("dp", "ctx", None),
        P(),
        P(),
        P("dp", "ctx", None),
        P("ctx", None, None, None),
    )
    out_specs = (
        P("dp", "ctx", None),
        P("dp", "ctx", None),
        P("dp", "ctx", None),
        P("ctx", "dp", None, None),
    )
    return jax.shard_map(
        per_device, mesh=mesh, in_specs=in_specs, out_specs=out_specs, check_vma=False
    )
```

```python
import math

import jax
import jax.numpy as jnp
from jax import lax
from jax.experimental import pallas as pl
from jax.experimental.pallas import tpu as pltpu
from jax.sharding import PartitionSpec as P

D = 4096
QUERY_HEADS = 32
KEY_VALUE_HEADS = 2
HEAD_SIZE = 128
TOP = 8
CAP = 12
H = 768
N_CTX = 16
N_CHIP = 8
ROWS = 128
KEYS = 2048
SLOTS = 16
FOLDS = 4
WIDE = D // FOLDS
SLAB = CAP * FOLDS
SLAB_ROWS = SLOTS * SLAB
PAIRS = QUERY_HEADS // 2
KEY_BLOCK = 512
PART = H // 8

MASK_FILLER = -1e30
EPSILON = 1e-06
INV_ROOT = HEAD_SIZE ** (-0.5)
TO_BASE_TWO = INV_ROOT * math.log2(math.e)

X_GROUPS = [[0, 1, 2, 3], [4, 5, 6, 7]]
MESH = pl.DeviceIdType.MESH
VMEM_LIMIT = 60 * 2**20
BF = jnp.bfloat16
F32 = jnp.float32


def dot_nn(a, b):
    return lax.dot_general(a, b, (((1,), (0,)), ((), ())), preferred_element_type=F32)


def dot_nt(a, b):
    return lax.dot_general(a, b, (((1,), (1,)), ((), ())), preferred_element_type=F32)


def dot_tn(a, b):
    return lax.dot_general(a, b, (((0,), (0,)), ((), ())), preferred_element_type=F32)


def in_vmem(count):
    return [pl.BlockSpec(memory_space=pltpu.VMEM)] * count


def local(cost):
    return dict(
        compiler_params=pltpu.CompilerParams(vmem_limit_bytes=VMEM_LIMIT),
        cost_estimate=pl.CostEstimate(flops=cost, bytes_accessed=2**22, transcendentals=0),
    )


def expert_ranks(ids_ref, trainable_ref):
    hits = jnp.zeros((SLOTS, ROWS), F32)
    for k in range(TOP):
        hits = hits + jnp.where(ids_ref[k : k + 1, :] == trainable_ref[...], 1.0, 0.0)
    before = lax.broadcasted_iota(jnp.int32, (ROWS, ROWS), 0) < lax.broadcasted_iota(
        jnp.int32, (ROWS, ROWS), 1
    )
    rank = dot_nn(hits.astype(BF), jnp.where(before, 1.0, 0.0).astype(BF))
    return jnp.where(hits > 0.5, rank, -1.0)


def tenth(n):
    return lax.shift_right_logical(n * 5462, 16)


def slot_mask(rank, pad):
    rows = SLOTS * pad
    n = lax.broadcasted_iota(jnp.int32, (rows, SLOTS), 0)
    j = lax.broadcasted_iota(jnp.int32, (rows, SLOTS), 1)
    owner = tenth(n) if pad == CAP else lax.shift_right_logical(n, 4)
    spread = dot_nn(jnp.where(owner == j, 1.0, 0.0).astype(BF), rank.astype(BF))
    slot = n[:, :1] - pad * owner[:, :1]
    return spread == slot.astype(F32), owner


def swap_mask():
    o = lax.broadcasted_iota(jnp.int32, (4 * SLAB, 4 * SLAB), 0)
    i = lax.broadcasted_iota(jnp.int32, (4 * SLAB, 4 * SLAB), 1)
    a = sum(jnp.where(o >= SLAB * k, 1, 0) for k in range(1, 4))
    o = o - SLAB * a
    b = sum(jnp.where(o >= CAP * k, 1, 0) for k in range(1, 4))
    return jnp.where(i == SLAB * b + CAP * a + o - CAP * b, 1.0, 0.0).astype(BF)


def unfolded(slabs, swap):
    for g in range(4):
        rows = dot_nn(swap, slabs[g * 4 * SLAB : (g + 1) * 4 * SLAB])
        for a in range(FOLDS):
            yield slice(g * SLAB, (g + 1) * SLAB), a, rows[a * SLAB : (a + 1) * SLAB]


def folded(rows, swap):
    wide = rows.shape[1] // FOLDS
    slabs = []
    for g in range(4):
        at = slice(g * SLAB, (g + 1) * SLAB)
        pile = [rows[at, a * wide : (a + 1) * wide] for a in range(FOLDS)]
        slabs.append(dot_nn(swap, jnp.concatenate(pile, axis=0)).astype(BF))
    return jnp.concatenate(slabs, axis=0)


def exact(a, b):
    return lax.dot_general(
        a, b, (((1,), (0,)), ((), ())),
        precision=lax.Precision.HIGHEST, preferred_element_type=F32,
    )


def weighted_kernel(ids_ref, gates_ref, trainable_ref, up_ref, out_ref):
    rank = expert_ranks(ids_ref, trainable_ref)
    mask, owner = slot_mask(rank, CAP)
    gates = jnp.zeros((SLOTS, ROWS), F32)
    for k in range(TOP):
        same = ids_ref[k : k + 1, :] == trainable_ref[...]
        gates = gates + jnp.where(same, gates_ref[k : k + 1, :], 0.0)
    own = owner == lax.broadcasted_iota(jnp.int32, owner.shape, 1)
    gates = exact(jnp.where(own, 1.0, 0.0), gates)
    gate = jnp.sum(jnp.where(mask, gates, 0.0), axis=1, keepdims=True)
    rows = dot_nn(jnp.where(mask, 1.0, 0.0).astype(BF), up_ref[...])
    out_ref[...] = folded((gate * rows).astype(BF), swap_mask())


def two_heads(ref, pair):
    at = pl.multiple_of(pair * 2 * HEAD_SIZE, 2 * HEAD_SIZE)
    both = ref[:, pl.ds(at, 2 * HEAD_SIZE)]
    return jnp.concatenate([both[:, :HEAD_SIZE], both[:, HEAD_SIZE:]], axis=0)


def put_two_heads(ref, pair, stacked):
    at = pl.multiple_of(pair * 2 * HEAD_SIZE, 2 * HEAD_SIZE)
    ref[:, pl.ds(at, 2 * HEAD_SIZE)] = jnp.concatenate([stacked[:ROWS], stacked[ROWS:]], axis=1)


def diagonal():
    eye = lax.broadcasted_iota(jnp.int32, (ROWS, ROWS), 0) == lax.broadcasted_iota(
        jnp.int32, (ROWS, ROWS), 1
    )
    one = jnp.where(eye, MASK_FILLER, 0.0).astype(BF)
    return jnp.concatenate([one, one], axis=0)


def rms_factor(features):
    return lax.rsqrt(jnp.mean(features * features, axis=1, keepdims=True) + EPSILON)


def forward_kernel(
    kv_ref, slabs_ref, q_ref, hidden_ref, ids_ref, trainable_ref,
    whole_ref, slabs_out_ref, mixed_ref, spread_ref, rows_ref, factors_ref,
    masked_keys, values_t, hides, scores, sent_rows, sent_factors,
    send_sem, recv_sem, pass_sem, passed_sem, near_sem, own_sem,
    slab_send, slab_recv, row_send, row_recv, row_own, factor_send, factor_recv,
):
    me = lax.axis_index("ctx")
    chip, core = lax.div(me, 2), lax.rem(me, 2)
    sibling = 2 * chip + 1 - core
    far = [2 * lax.rem(chip + d, N_CHIP) + core for d in range(1, N_CHIP)]
    others = [lax.rem(me + d, N_CTX) for d in range(1, N_CTX)]
    greet(others)
    copies = []
    for d, other in enumerate(far):
        copy = send(kv_ref, whole_ref.at[me], send_sem.at[d], recv_sem.at[d], other)
        copy.start()
        copies.append(copy)
    near = send(kv_ref, whole_ref.at[me], near_sem.at[0], near_sem.at[1], sibling)
    near.start()
    own = pltpu.make_async_copy(kv_ref, whole_ref.at[me], own_sem.at[0])
    own.start()

    mask, _ = slot_mask(expert_ranks(ids_ref, trainable_ref), CAP)
    mask = jnp.where(mask, 1.0, 0.0).astype(BF)
    swap = swap_mask()
    hides[...] = diagonal()
    for g in range(KEY_VALUE_HEADS):
        masked_keys[g, :, HEAD_SIZE:] = hidden_ref[...]

    passed = []
    for d in range(1, N_CHIP):
        source = 2 * lax.rem(chip + N_CHIP - d, N_CHIP) + core
        copies[d - 1].wait_recv()
        copy = send(
            whole_ref.at[source], whole_ref.at[source],
            pass_sem.at[d - 1], passed_sem.at[d - 1], sibling,
        )
        copy.start()
        passed.append(copy)
    for copy in copies:
        copy.wait_send()
    near.wait()
    own.wait()
    for copy in passed:
        copy.wait()

    slabs = []
    for d, other in enumerate(others):
        copy = send(
            slabs_ref.at[other], slabs_out_ref.at[me], slab_send.at[d], slab_recv.at[d], other
        )
        copy.start()
        slabs.append(copy)
    own_slab = pltpu.make_async_copy(slabs_ref.at[me], slabs_out_ref.at[me], own_sem.at[1])
    own_slab.start()

    for g in range(KEY_VALUE_HEADS):
        at = g * HEAD_SIZE
        keys = whole_ref[:, :, at : at + HEAD_SIZE].reshape(KEYS, HEAD_SIZE)
        masked_keys[g, :, :HEAD_SIZE] = keys
        at = (KEY_VALUE_HEADS + g) * HEAD_SIZE
        values_t[g] = whole_ref[:, :, at : at + HEAD_SIZE].reshape(KEYS, HEAD_SIZE).T

    def step(pair, carry):
        g = lax.div(pair, PAIRS // KEY_VALUE_HEADS)
        queries = jnp.concatenate([two_heads(q_ref, pair), hides[...]], axis=1)
        peak = None
        for b in range(KEYS // KEY_BLOCK):
            rows = slice(b * KEY_BLOCK, (b + 1) * KEY_BLOCK)
            block = dot_nt(masked_keys[g, rows, :], queries)
            scores[rows, :] = block
            top = jnp.max(block, axis=0, keepdims=True)
            peak = top if peak is None else jnp.maximum(peak, top)
        total, out = None, None
        for b in range(KEYS // KEY_BLOCK):
            rows = slice(b * KEY_BLOCK, (b + 1) * KEY_BLOCK)
            exps = jnp.exp2((scores[rows, :] - peak) * TO_BASE_TWO)
            part = jnp.sum(exps, axis=0, keepdims=True)
            piece = dot_nn(values_t[g, :, rows], exps.astype(BF))
            total = part if total is None else total + part
            out = piece if out is None else out + piece
        put_two_heads(mixed_ref, pair, (out / total).T.astype(BF))
        spread_ref[pl.ds(pair, 1), :] = peak * TO_BASE_TWO + jnp.log2(total)
        return carry

    def row_copies(f):
        return [
            send(
                sent_rows.at[f, other], rows_ref.at[f, me],
                row_send.at[f, d], row_recv.at[f, d], other,
            )
            for d, other in enumerate(others)
        ]

    def own_rows(f):
        return pltpu.make_async_copy(sent_rows.at[f, me], rows_ref.at[f, me], row_own.at[f])

    def quarter(f, carry):
        lax.fori_loop(f * (PAIRS // FOLDS), (f + 1) * (PAIRS // FOLDS), step, 0)
        columns = mixed_ref[:, pl.ds(pl.multiple_of(f * WIDE, WIDE), WIDE)]
        picked = folded(dot_nn(mask, columns).astype(BF), swap)
        sent_rows[f] = picked.reshape(SLOTS, SLAB, WIDE // FOLDS)
        for copy in row_copies(f):
            copy.start()
        own_rows(f).start()
        return carry

    lax.fori_loop(0, FOLDS, quarter, 0)

    features = mixed_ref[...].astype(F32)
    factor = jnp.broadcast_to(rms_factor(features), (ROWS, 128))
    padded, _ = slot_mask(expert_ranks(ids_ref, trainable_ref), 16)
    picked = exact(jnp.where(padded, 1.0, 0.0), factor)
    sent_factors[...] = picked.reshape(SLOTS, 16, 128)
    factors = []
    for d, other in enumerate(others):
        copy = send(
            sent_factors.at[other], factors_ref.at[me], factor_send.at[d], factor_recv.at[d], other
        )
        copy.start()
        factors.append(copy)
    own_factor = pltpu.make_async_copy(sent_factors.at[me], factors_ref.at[me], own_sem.at[2])
    own_factor.start()

    for copy in slabs:
        copy.wait()
    own_slab.wait()

    def finish(f, carry):
        for copy in row_copies(f):
            copy.wait()
        own_rows(f).wait()
        return carry

    lax.fori_loop(0, FOLDS, finish, 0)
    for copy in factors:
        copy.wait()
    own_factor.wait()


def unfold_kernel(slab_ref, out_ref):
    for rows, a, values in unfolded(slab_ref[...], swap_mask()):
        out_ref[rows, a * WIDE : (a + 1) * WIDE] = values.astype(BF)


def norm_kernel(rows_ref, factors_ref, gain_ref, out_ref):
    n = lax.broadcasted_iota(jnp.int32, (SLOTS * CAP, SLOTS * 16), 0)
    m = lax.broadcasted_iota(jnp.int32, (SLOTS * CAP, SLOTS * 16), 1)
    kept = jnp.where(m == n + (16 - CAP) * tenth(n), 1.0, 0.0)
    factor = exact(kept, factors_ref[...])[:, :1]
    swap = swap_mask()
    narrow = WIDE // FOLDS
    for f in range(FOLDS):
        for rows, a, values in unfolded(rows_ref[f], swap):
            at = f * WIDE + a * narrow
            gain = gain_ref[:, at : at + narrow]
            out_ref[rows, at : at + narrow] = (values * factor[rows] * gain).astype(BF)


def expert_kernel(
    mine_ref, rows_ref, grads_ref, w_ref, terms_ref, products_ref, back_ref,
    routed_t, weighted_t, returned,
):
    step = pl.program_id(0)

    @pl.when(step == 0)
    def _():
        routed_t[...] = rows_ref[...].T
        weighted_t[...] = grads_ref[...].T

    gate_in = dot_nn(w_ref[0], routed_t[...])
    up_in = dot_nn(w_ref[1], routed_t[...])
    back = dot_nn(w_ref[2], weighted_t[...])
    sigma = jax.nn.sigmoid(gate_in)
    activated = gate_in * sigma
    grad_gate = (back * up_in * sigma * (1.0 + gate_in * (1.0 - sigma))).astype(BF)
    grad_up = (back * activated).astype(BF)
    place = lax.rem(step + mine_ref[0], 2)
    products_ref[place] = (activated * up_in).astype(BF)
    for x in range(4):
        terms_ref[x, place, 0] = grad_gate[x * PART : (x + 1) * PART]
        terms_ref[x, place, 1] = grad_up[x * PART : (x + 1) * PART]
    grad_gate, grad_up = grad_gate.T, grad_up.T
    for f in range(FOLDS):
        at = slice(f * WIDE, (f + 1) * WIDE)
        part = dot_nn(grad_gate, w_ref[0, :, at]) + dot_nn(grad_up, w_ref[1, :, at])

        @pl.when(step == 0)
        def _():
            returned[:, at] = part

        @pl.when(step > 0)
        def _():
            returned[:, at] += part

    @pl.when(step == pl.num_programs(0) - 1)
    def _():
        back_ref[...] = folded(returned[...].astype(BF), swap_mask())


def down_kernel(own_ref, other_ref, own_products_ref, other_products_ref, out_ref):
    out_ref[...] = (
        dot_nn(own_products_ref[...], own_ref[...])
        + dot_nn(other_products_ref[...], other_ref[...])
    ).astype(BF)


def gate_up_kernel(terms0, terms1, terms2, terms3, rows_ref, kept_ref, given_ref):
    x = lax.rem(lax.axis_index("dp"), 4)
    total = None
    for k, terms in enumerate((terms0, terms1, terms2, terms3)):
        left = terms[...].reshape(4 * PART, SLOTS * CAP)
        part = dot_nn(left, rows_ref[lax.rem(x + 4 - k, 4)])
        total = part if total is None else total + part
    kept_ref[...] = total[: 2 * PART].astype(BF)
    given_ref[...] = total[2 * PART :].astype(BF)


def fill_keys(kv_ref, hidden_ref, g, masked_keys, keys_t, hides):
    keys = kv_ref[:, g * HEAD_SIZE : (g + 1) * HEAD_SIZE]
    masked_keys[:, :HEAD_SIZE] = keys
    masked_keys[:, HEAD_SIZE:] = hidden_ref[...]
    keys_t[...] = keys.T
    hides[...] = diagonal()


def backward_pairs(
    g, q_ref, kv_ref, mixed_ref, spread_ref, grad_mixed_ref, d_query_ref,
    masked_keys, keys_t, hides, key_sums, value_sums,
):
    count = PAIRS // KEY_VALUE_HEADS
    skip = g * count - (d_query_ref.shape[1] // (2 * HEAD_SIZE) - count)
    key_sums[...] = jnp.zeros_like(key_sums)
    value_sums[...] = jnp.zeros_like(value_sums)
    at = (KEY_VALUE_HEADS + g) * HEAD_SIZE

    def step(pair, carry):
        plain = two_heads(q_ref, pair)
        queries = jnp.concatenate([plain, hides[...]], axis=1)
        grads = two_heads(grad_mixed_ref, pair)
        products = grads.astype(F32) * two_heads(mixed_ref, pair).astype(F32)
        delta = jnp.sum(products.T, axis=0, keepdims=True)
        spread = spread_ref[pl.ds(pair, 1), :]
        d_query = None
        for b in range(KEYS // KEY_BLOCK):
            rows = slice(b * KEY_BLOCK, (b + 1) * KEY_BLOCK)
            values = kv_ref[rows, at : at + HEAD_SIZE]
            raw = dot_nt(masked_keys[rows, :], queries)
            probs = jnp.exp2(raw * TO_BASE_TWO - spread)
            pushed = dot_nt(values, grads)
            slopes = (probs * (pushed - delta)).astype(BF)
            value_sums[rows, :] += dot_nn(probs.astype(BF), grads)
            key_sums[rows, :] += dot_nn(slopes, plain)
            piece = dot_nn(keys_t[:, rows], slopes)
            d_query = piece if d_query is None else d_query + piece
        put_two_heads(d_query_ref, pair - skip, (d_query * INV_ROOT).T.astype(BF))
        return carry

    lax.fori_loop(g * count, (g + 1) * count, step, 0)


def first_backward_kernel(
    q_ref, kv_ref, hidden_ref, ids_ref, trainable_ref, gain_ref,
    mixed_ref, spread_ref, up_ref, echo_ref,
    d_query_ref, d_kv_ref, grad_mixed_ref,
    masked_keys, keys_t, hides, key_sums, value_sums, echoed,
):
    mask, _ = slot_mask(expert_ranks(ids_ref, trainable_ref), CAP)
    mask = jnp.where(mask, 1.0, 0.0).astype(BF)
    for rows, a, values in unfolded(echo_ref[...], swap_mask()):
        echoed[rows, a * WIDE : (a + 1) * WIDE] = values.astype(BF)
    features = mixed_ref[...].astype(F32)
    factor = rms_factor(features)
    gradnorm = gain_ref[...] * dot_tn(mask, echoed[...])
    across = jnp.mean(gradnorm * features, axis=1, keepdims=True)
    grad_mixed_ref[...] = (
        up_ref[...].astype(F32)
        + factor * gradnorm
        - features * (factor * factor * factor) * across
    ).astype(BF)
    fill_keys(kv_ref, hidden_ref, 0, masked_keys, keys_t, hides)
    backward_pairs(
        0, q_ref, kv_ref, mixed_ref, spread_ref, grad_mixed_ref, d_query_ref,
        masked_keys, keys_t, hides, key_sums, value_sums,
    )
    d_kv_ref[:, :HEAD_SIZE] = (key_sums[...] * INV_ROOT).astype(BF)
    d_kv_ref[:, HEAD_SIZE:] = value_sums[...].astype(BF)


def second_backward_kernel(
    q_ref, kv_ref, hidden_ref, mixed_ref, spread_ref, grad_mixed_ref, first_query_ref, first_kv_ref,
    d_query_ref, d_kv_ref,
    masked_keys, keys_t, hides, key_sums, value_sums,
):
    d_query_ref[:, : D // 2] = first_query_ref[...]
    d_kv_ref[:, :HEAD_SIZE] = first_kv_ref[:, :HEAD_SIZE]
    d_kv_ref[:, 2 * HEAD_SIZE : 3 * HEAD_SIZE] = first_kv_ref[:, HEAD_SIZE:]
    fill_keys(kv_ref, hidden_ref, 1, masked_keys, keys_t, hides)
    backward_pairs(
        1, q_ref, kv_ref, mixed_ref, spread_ref, grad_mixed_ref, d_query_ref,
        masked_keys, keys_t, hides, key_sums, value_sums,
    )
    d_kv_ref[:, HEAD_SIZE : 2 * HEAD_SIZE] = (key_sums[...] * INV_ROOT).astype(BF)
    d_kv_ref[:, 3 * HEAD_SIZE :] = value_sums[...].astype(BF)


def greet(targets):
    barrier = pltpu.get_barrier_semaphore()
    for target in targets:
        pl.semaphore_signal(barrier, inc=1, device_id={"ctx": target}, device_id_type=MESH)
    pl.semaphore_wait(barrier, len(targets))


def send(source, target, send_sem, recv_sem, device):
    return pltpu.make_async_remote_copy(
        src_ref=source, dst_ref=target, send_sem=send_sem, recv_sem=recv_sem,
        device_id={"ctx": device}, device_id_type=MESH,
    )


def exchange_kernel(x_ref, out_ref, send_sem, recv_sem, own_sem):
    me = lax.axis_index("ctx")
    others = [lax.rem(me + d, N_CTX) for d in range(1, N_CTX)]
    greet(others)
    copies = []
    for d, other in enumerate(others):
        copy = send(x_ref.at[other], out_ref.at[me], send_sem.at[d], recv_sem.at[d], other)
        copy.start()
        copies.append(copy)
    own = pltpu.make_async_copy(x_ref.at[me], out_ref.at[me], own_sem)
    own.start()
    for copy in copies:
        copy.wait()
    own.wait()


def scatter_kernel(
    x_ref, out_ref, near, sums, landed, near_send, near_recv, send_sem, recv_sem
):
    me = lax.axis_index("ctx")
    chip, core = lax.div(me, 2), lax.rem(me, 2)
    sibling = 2 * chip + 1 - core
    chips = [lax.rem(chip + d, N_CHIP) for d in range(N_CHIP)]
    greet([*(2 * c + core for c in chips[1:]), sibling])
    order = [*range(1, N_CHIP), 0]
    shared = {}
    for d in order:
        copy = send(
            x_ref.at[2 * chips[d] + 1 - core], near.at[d], near_send.at[d], near_recv.at[d], sibling
        )
        copy.start()
        shared[d] = copy
    copies = []
    for d in order:
        shared[d].wait_recv()
        both = x_ref[2 * chips[d] + core].astype(F32) + near[d].astype(F32)
        if d == 0:
            total = both
        else:
            sums[d] = both.astype(BF)
            copy = send(
                sums.at[d], landed.at[d], send_sem.at[d], recv_sem.at[d], 2 * chips[d] + core
            )
            copy.start()
            copies.append(copy)
    for d, copy in enumerate(copies, start=1):
        copy.wait_recv()
        total = total + landed[d].astype(F32)
    out_ref[...] = total.astype(BF)
    for copy in copies:
        copy.wait_send()
    for d in order:
        shared[d].wait_send()


def dma(count):
    return pltpu.SemaphoreType.DMA((count,))


def remote(kernel, shape, scratch, number, sent):
    return pl.pallas_call(
        kernel,
        out_shape=jax.ShapeDtypeStruct(shape, BF),
        in_specs=in_vmem(1),
        out_specs=in_vmem(1)[0],
        scratch_shapes=scratch,
        compiler_params=pltpu.CompilerParams(
            collective_id=number, has_side_effects=True, vmem_limit_bytes=VMEM_LIMIT
        ),
        cost_estimate=pl.CostEstimate(flops=0, bytes_accessed=sent, transcendentals=0),
    )


def exchange(slabs, number):
    shape = (SLOTS, SLAB, WIDE)
    scratch = [dma(N_CTX - 1), dma(N_CTX - 1), pltpu.SemaphoreType.DMA]
    out = remote(exchange_kernel, shape, scratch, number, 2**26)(slabs.reshape(shape))
    return out.reshape(SLAB_ROWS, WIDE)


def scatter_sum(parts):
    blocks = parts.reshape(N_CTX, ROWS, -1)
    block = blocks.shape[1:]
    slots = pltpu.VMEM((N_CHIP, *block), BF)
    scratch = [slots, slots, slots, dma(8), dma(8), dma(8), dma(8)]
    return remote(scatter_kernel, block, scratch, 3, 2**26)(blocks)


def over_pair(array):
    return lax.ppermute(array, "dp", [(i, (i + 4) % 8) for i in range(8)])


def unfold(slab, name):
    return pl.pallas_call(
        unfold_kernel,
        out_shape=jax.ShapeDtypeStruct((SLOTS * CAP, D), BF),
        in_specs=in_vmem(1),
        out_specs=in_vmem(1)[0],
        name=name,
        **local(10**9),
    )(slab)


def per_device(
    query, key, value, span_order, expert_ids, expert_gates,
    trainable, norm_gain, upstream, expert_weights,
):
    bf_shape = lambda *s: jax.ShapeDtypeStruct(s, BF)
    half = ROWS // 2
    place = (span_order[0][:, None] * half + jnp.arange(half, dtype=jnp.int32)[None, :]).reshape(-1)
    own_place = lax.dynamic_slice_in_dim(place, lax.axis_index("ctx") * ROWS, ROWS)
    hidden = (place[:, None] > own_place[None, :]).astype(BF)
    ids, named = expert_ids[0].T, trainable[:, None]
    gain = norm_gain[None, :]
    weights = expert_weights[0].transpose(1, 0, 2)

    slab_shape = bf_shape(SLAB_ROWS, WIDE)
    sent_grads = pl.pallas_call(
        weighted_kernel, out_shape=slab_shape, in_specs=in_vmem(4), out_specs=in_vmem(1)[0],
        name="weighted", **local(10**9),
    )(ids, expert_gates[0].T, named, upstream[0])

    groups = KEY_VALUE_HEADS
    slabs = (SLOTS, SLAB, WIDE)
    quarters = (FOLDS, SLOTS, SLAB, WIDE // FOLDS)
    factor_shape = jax.ShapeDtypeStruct((SLOTS, 16, 128), F32)
    whole, grad_slabs, mixed, spread, row_slabs, factors = pl.pallas_call(
        forward_kernel,
        out_shape=(
            bf_shape(N_CTX, ROWS, 2 * groups * HEAD_SIZE),
            bf_shape(*slabs),
            bf_shape(ROWS, D),
            jax.ShapeDtypeStruct((PAIRS, 2 * ROWS), F32),
            bf_shape(*quarters),
            factor_shape,
        ),
        in_specs=in_vmem(6),
        out_specs=tuple(in_vmem(6)),
        scratch_shapes=[
            pltpu.VMEM((groups, KEYS, 2 * HEAD_SIZE), BF),
            pltpu.VMEM((groups, HEAD_SIZE, KEYS), BF),
            pltpu.VMEM((2 * ROWS, ROWS), BF),
            pltpu.VMEM((KEYS, 2 * ROWS), F32),
            pltpu.VMEM(quarters, BF),
            pltpu.VMEM((SLOTS, 16, 128), F32),
            dma(7), dma(7), dma(7), dma(7), dma(2), dma(3), dma(15), dma(15),
            pltpu.SemaphoreType.DMA((FOLDS, 15)), pltpu.SemaphoreType.DMA((FOLDS, 15)),
            dma(FOLDS), dma(15), dma(15),
        ],
        compiler_params=pltpu.CompilerParams(
            collective_id=0, has_side_effects=True, vmem_limit_bytes=VMEM_LIMIT
        ),
        cost_estimate=pl.CostEstimate(flops=2 * 10**10, bytes_accessed=2**26, transcendentals=0),
        name="attention",
    )(
        jnp.concatenate([key[0], value[0]], axis=1), sent_grads.reshape(slabs),
        query[0], hidden, ids, named,
    )
    whole = whole.reshape(KEYS, -1)
    grad_slabs = grad_slabs.reshape(SLAB_ROWS, WIDE)
    other_slabs = over_pair(grad_slabs)

    rows = pl.pallas_call(
        norm_kernel, out_shape=bf_shape(SLOTS * CAP, D), in_specs=in_vmem(3),
        out_specs=in_vmem(1)[0], name="unfold_rows", **local(10**9),
    )(
        row_slabs.reshape(FOLDS, SLAB_ROWS, WIDE // FOLDS), factors.reshape(SLOTS * 16, 128), gain
    )
    all_rows = lax.all_gather(rows, "dp", axis=0, axis_index_groups=X_GROUPS)
    grads = unfold(grad_slabs, "unfold_grads")

    mine = lax.div(lax.axis_index("dp"), 4)
    half, taken_rows = H // 2, SLOTS * CAP
    terms, products, sent_back = pl.pallas_call(
        expert_kernel,
        grid=(2,),
        out_shape=(
            bf_shape(4, 2, 2, PART, taken_rows),
            bf_shape(2, half, taken_rows),
            slab_shape,
        ),
        in_specs=[
            pl.BlockSpec(memory_space=pltpu.SMEM),
            pl.BlockSpec((taken_rows, D), lambda i: (0, 0)),
            pl.BlockSpec((taken_rows, D), lambda i: (0, 0)),
            pl.BlockSpec((3, half, D), lambda i: (0, i, 0)),
        ],
        out_specs=(
            pl.BlockSpec((4, 2, 2, PART, taken_rows), lambda i: (0, 0, 0, 0, 0)),
            pl.BlockSpec((2, half, taken_rows), lambda i: (0, 0, 0)),
            pl.BlockSpec((SLAB_ROWS, WIDE), lambda i: (0, 0)),
        ),
        scratch_shapes=[
            pltpu.VMEM((D, taken_rows), BF),
            pltpu.VMEM((D, taken_rows), BF),
            pltpu.VMEM((taken_rows, D), F32),
        ],
        name="experts",
        **local(10**10),
    )(mine[None], rows, grads, weights)

    x = lax.rem(lax.axis_index("dp"), 4)
    near_terms = [lax.dynamic_index_in_dim(terms, x, 0, keepdims=False)]
    for k in range(1, 4):
        given = lax.dynamic_index_in_dim(terms, lax.rem(x + k, 4), 0, keepdims=False)
        near_terms.append(
            lax.ppermute(given, "dp", [(i, 4 * (i // 4) + (i + k) % 4) for i in range(8)])
        )
    other_products = over_pair(products[1])

    echo = exchange(sent_back, 2)
    other_grads = unfold(other_slabs, "unfold_others")
    other_products, products, echo, *near_terms = lax.optimization_barrier(
        (other_products, products, echo, *near_terms)
    )
    across = lambda rows: pl.BlockSpec((rows, WIDE), lambda i: (0, i))
    fixed = lambda *shape: pl.BlockSpec(shape, lambda i: (0,) * len(shape))
    down = pl.pallas_call(
        down_kernel,
        grid=(FOLDS,),
        out_shape=bf_shape(half, D),
        in_specs=[across(taken_rows), across(taken_rows), *[fixed(half, taken_rows)] * 2],
        out_specs=across(half),
        name="down_terms",
        **local(4 * 10**9),
    )(grads, other_grads, products[0], other_products)
    down = lax.psum_scatter(
        down, "dp", scatter_dimension=0, tiled=True, axis_index_groups=X_GROUPS
    )

    kept_scratch = [
        pltpu.VMEM((KEYS, 2 * HEAD_SIZE), BF),
        pltpu.VMEM((HEAD_SIZE, KEYS), BF),
        pltpu.VMEM((2 * ROWS, ROWS), BF),
        pltpu.VMEM((KEYS, HEAD_SIZE), F32),
        pltpu.VMEM((KEYS, HEAD_SIZE), F32),
    ]
    first_query, first_kv, grad_mixed = pl.pallas_call(
        first_backward_kernel,
        out_shape=(bf_shape(ROWS, D // 2), bf_shape(KEYS, 2 * HEAD_SIZE), bf_shape(ROWS, D)),
        in_specs=in_vmem(10),
        out_specs=tuple(in_vmem(3)),
        scratch_shapes=[*kept_scratch, pltpu.VMEM((SLOTS * CAP, D), BF)],
        name="attention_grads_0",
        **local(2 * 10**10),
    )(query[0], whole, hidden, ids, named, gain, mixed, spread, upstream[0], echo)
    first_kv, all_rows, *near_terms = lax.optimization_barrier((first_kv, all_rows, *near_terms))
    kept, given = pl.pallas_call(
        gate_up_kernel,
        grid=(FOLDS,),
        out_shape=(bf_shape(2 * PART, D), bf_shape(2 * PART, D)),
        in_specs=[
            *[fixed(2, 2, PART, taken_rows)] * 4,
            pl.BlockSpec((4, taken_rows, WIDE), lambda i: (0, 0, i)),
        ],
        out_specs=(across(2 * PART), across(2 * PART)),
        name="gate_up_terms",
        **local(4 * 10**9),
    )(*near_terms, all_rows)
    taken = over_pair(given)
    first_query, kept = lax.optimization_barrier((first_query, kept))
    d_query, d_kv = pl.pallas_call(
        second_backward_kernel,
        out_shape=(bf_shape(ROWS, D), bf_shape(KEYS, 2 * groups * HEAD_SIZE)),
        in_specs=in_vmem(8),
        out_specs=tuple(in_vmem(2)),
        scratch_shapes=kept_scratch,
        name="attention_grads_1",
        **local(2 * 10**10),
    )(query[0], whole, hidden, mixed, spread, grad_mixed, first_query, first_kv)
    kv_sums = scatter_sum(d_kv)
    split = groups * HEAD_SIZE
    gate_up = (kept.astype(F32) + taken.astype(F32)).astype(BF)
    expert_grads = jnp.concatenate([gate_up, down], axis=0).reshape(3, PART, D)
    return (
        d_query[None],
        kv_sums[None, :, :split],
        kv_sums[None, :, split:],
        expert_grads.transpose(1, 0, 2)[None],
    )


def solution(mesh):
    in_specs = (
        P("dp", "ctx", None),
        P("dp", "ctx", None),
        P("dp", "ctx", None),
        P("dp", None),
        P("dp", "ctx", None),
        P("dp", "ctx", None),
        P(),
        P(),
        P("dp", "ctx", None),
        P("ctx", None, None, None),
    )
    out_specs = (
        P("dp", "ctx", None),
        P("dp", "ctx", None),
        P("dp", "ctx", None),
        P("ctx", "dp", None, None),
    )
    return jax.shard_map(
        per_device, mesh=mesh, in_specs=in_specs, out_specs=out_specs, check_vma=False
    )
```

```python
import math

import jax
import jax.numpy as jnp
from jax import lax
from jax.experimental import pallas as pl
from jax.experimental.pallas import tpu as pltpu
from jax.sharding import PartitionSpec as P

D = 4096
QUERY_HEADS = 32
KEY_VALUE_HEADS = 2
HEAD_SIZE = 128
TOP = 8
CAP = 12
H = 768
N_CTX = 16
N_CHIP = 8
ROWS = 128
KEYS = 2048
SLOTS = 16
FOLDS = 4
WIDE = D // FOLDS
SLAB = CAP * FOLDS
SLAB_ROWS = SLOTS * SLAB
PAIRS = QUERY_HEADS // 2
KEY_BLOCK = 512
PART = H // 8

MASK_FILLER = -1e30
EPSILON = 1e-06
INV_ROOT = HEAD_SIZE ** (-0.5)
TO_BASE_TWO = INV_ROOT * math.log2(math.e)

X_GROUPS = [[0, 1, 2, 3], [4, 5, 6, 7]]
MESH = pl.DeviceIdType.MESH
VMEM_LIMIT = 40 * 2**20
BF = jnp.bfloat16
F32 = jnp.float32


def dot_nn(a, b):
    return lax.dot_general(a, b, (((1,), (0,)), ((), ())), preferred_element_type=F32)


def dot_nt(a, b):
    return lax.dot_general(a, b, (((1,), (1,)), ((), ())), preferred_element_type=F32)


def dot_tn(a, b):
    return lax.dot_general(a, b, (((0,), (0,)), ((), ())), preferred_element_type=F32)


def in_vmem(count):
    return [pl.BlockSpec(memory_space=pltpu.VMEM)] * count


def local(cost, limit=40):
    return dict(
        compiler_params=pltpu.CompilerParams(vmem_limit_bytes=limit * 2**20),
        cost_estimate=pl.CostEstimate(flops=cost, bytes_accessed=2**22, transcendentals=0),
    )


def expert_ranks(ids_ref, trainable_ref):
    hits = jnp.zeros((SLOTS, ROWS), F32)
    for k in range(TOP):
        hits = hits + jnp.where(ids_ref[k : k + 1, :] == trainable_ref[...], 1.0, 0.0)
    before = lax.broadcasted_iota(jnp.int32, (ROWS, ROWS), 0) < lax.broadcasted_iota(
        jnp.int32, (ROWS, ROWS), 1
    )
    rank = dot_nn(hits.astype(BF), jnp.where(before, 1.0, 0.0).astype(BF))
    return jnp.where(hits > 0.5, rank, -1.0)


def tenth(n):
    return lax.shift_right_logical(n * 5462, 16)


def slot_mask(rank, pad):
    rows = SLOTS * pad
    n = lax.broadcasted_iota(jnp.int32, (rows, SLOTS), 0)
    j = lax.broadcasted_iota(jnp.int32, (rows, SLOTS), 1)
    owner = tenth(n) if pad == CAP else lax.shift_right_logical(n, 4)
    spread = dot_nn(jnp.where(owner == j, 1.0, 0.0).astype(BF), rank.astype(BF))
    slot = n[:, :1] - pad * owner[:, :1]
    return spread == slot.astype(F32), owner


def swap_mask():
    o = lax.broadcasted_iota(jnp.int32, (4 * SLAB, 4 * SLAB), 0)
    i = lax.broadcasted_iota(jnp.int32, (4 * SLAB, 4 * SLAB), 1)
    a = sum(jnp.where(o >= SLAB * k, 1, 0) for k in range(1, 4))
    o = o - SLAB * a
    b = sum(jnp.where(o >= CAP * k, 1, 0) for k in range(1, 4))
    return jnp.where(i == SLAB * b + CAP * a + o - CAP * b, 1.0, 0.0).astype(BF)


def unfolded(slabs, swap):
    for g in range(4):
        rows = dot_nn(swap, slabs[g * 4 * SLAB : (g + 1) * 4 * SLAB])
        for a in range(FOLDS):
            yield slice(g * SLAB, (g + 1) * SLAB), a, rows[a * SLAB : (a + 1) * SLAB]


def folded(rows, swap):
    wide = rows.shape[1] // FOLDS
    slabs = []
    for g in range(4):
        at = slice(g * SLAB, (g + 1) * SLAB)
        pile = [rows[at, a * wide : (a + 1) * wide] for a in range(FOLDS)]
        slabs.append(dot_nn(swap, jnp.concatenate(pile, axis=0)).astype(BF))
    return jnp.concatenate(slabs, axis=0)


def exact(a, b):
    return lax.dot_general(
        a, b, (((1,), (0,)), ((), ())),
        precision=lax.Precision.HIGHEST, preferred_element_type=F32,
    )


def weighted_kernel(ids_ref, gates_ref, trainable_ref, up_ref, out_ref):
    rank = expert_ranks(ids_ref, trainable_ref)
    mask, owner = slot_mask(rank, CAP)
    gates = jnp.zeros((SLOTS, ROWS), F32)
    for k in range(TOP):
        same = ids_ref[k : k + 1, :] == trainable_ref[...]
        gates = gates + jnp.where(same, gates_ref[k : k + 1, :], 0.0)
    own = owner == lax.broadcasted_iota(jnp.int32, owner.shape, 1)
    gates = exact(jnp.where(own, 1.0, 0.0), gates)
    gate = jnp.sum(jnp.where(mask, gates, 0.0), axis=1, keepdims=True)
    rows = dot_nn(jnp.where(mask, 1.0, 0.0).astype(BF), up_ref[...])
    out_ref[...] = folded((gate * rows).astype(BF), swap_mask())


def two_heads(ref, pair):
    at = pl.multiple_of(pair * 2 * HEAD_SIZE, 2 * HEAD_SIZE)
    both = ref[:, pl.ds(at, 2 * HEAD_SIZE)]
    return jnp.concatenate([both[:, :HEAD_SIZE], both[:, HEAD_SIZE:]], axis=0)


def put_two_heads(ref, pair, stacked):
    at = pl.multiple_of(pair * 2 * HEAD_SIZE, 2 * HEAD_SIZE)
    ref[:, pl.ds(at, 2 * HEAD_SIZE)] = jnp.concatenate([stacked[:ROWS], stacked[ROWS:]], axis=1)


def diagonal():
    eye = lax.broadcasted_iota(jnp.int32, (ROWS, ROWS), 0) == lax.broadcasted_iota(
        jnp.int32, (ROWS, ROWS), 1
    )
    one = jnp.where(eye, MASK_FILLER, 0.0).astype(BF)
    return jnp.concatenate([one, one], axis=0)


def rms_factor(features):
    return lax.rsqrt(jnp.mean(features * features, axis=1, keepdims=True) + EPSILON)


def forward_kernel(
    kv_ref, slabs_ref, q_ref, hidden_ref, ids_ref, trainable_ref, gain_ref,
    whole_ref, mixed_ref, spread_ref, rows_ref, grads_ref,
    masked_keys, values_t, hides, scores, sent_rows, sent_factors, slabs_in, rows_in, factors_in,
    send_sem, recv_sem, pass_sem, passed_sem, near_sem, own_sem,
    slab_send, slab_recv, row_send, row_recv, row_own, factor_send, factor_recv,
):
    me = lax.axis_index("ctx")
    chip, core = lax.div(me, 2), lax.rem(me, 2)
    sibling = 2 * chip + 1 - core
    far = [2 * lax.rem(chip + d, N_CHIP) + core for d in range(1, N_CHIP)]
    others = [lax.rem(me + d, N_CTX) for d in range(1, N_CTX)]
    greet(others)
    copies = []
    for d, other in enumerate(far):
        copy = send(kv_ref, whole_ref.at[me], send_sem.at[d], recv_sem.at[d], other)
        copy.start()
        copies.append(copy)
    near = send(kv_ref, whole_ref.at[me], near_sem.at[0], near_sem.at[1], sibling)
    near.start()
    own = pltpu.make_async_copy(kv_ref, whole_ref.at[me], own_sem.at[0])
    own.start()

    mask, _ = slot_mask(expert_ranks(ids_ref, trainable_ref), CAP)
    mask = jnp.where(mask, 1.0, 0.0).astype(BF)
    swap = swap_mask()
    hides[...] = diagonal()
    for g in range(KEY_VALUE_HEADS):
        masked_keys[g, :, HEAD_SIZE:] = hidden_ref[...]

    passed = []
    for d in range(1, N_CHIP):
        source = 2 * lax.rem(chip + N_CHIP - d, N_CHIP) + core
        copies[d - 1].wait_recv()
        copy = send(
            whole_ref.at[source], whole_ref.at[source],
            pass_sem.at[d - 1], passed_sem.at[d - 1], sibling,
        )
        copy.start()
        passed.append(copy)
    for copy in copies:
        copy.wait_send()
    near.wait()
    own.wait()
    for copy in passed:
        copy.wait()

    slabs = []
    for d, other in enumerate(others):
        copy = send(
            slabs_ref.at[other], slabs_in.at[me], slab_send.at[d], slab_recv.at[d], other
        )
        copy.start()
        slabs.append(copy)
    own_slab = pltpu.make_async_copy(slabs_ref.at[me], slabs_in.at[me], own_sem.at[1])
    own_slab.start()

    for g in range(KEY_VALUE_HEADS):
        at = g * HEAD_SIZE
        keys = whole_ref[:, :, at : at + HEAD_SIZE].reshape(KEYS, HEAD_SIZE)
        masked_keys[g, :, :HEAD_SIZE] = keys
        at = (KEY_VALUE_HEADS + g) * HEAD_SIZE
        values_t[g] = whole_ref[:, :, at : at + HEAD_SIZE].reshape(KEYS, HEAD_SIZE).T

    def step(pair, carry):
        g = lax.div(pair, PAIRS // KEY_VALUE_HEADS)
        queries = jnp.concatenate([two_heads(q_ref, pair), hides[...]], axis=1)
        peak = None
        for b in range(KEYS // KEY_BLOCK):
            rows = slice(b * KEY_BLOCK, (b + 1) * KEY_BLOCK)
            block = dot_nt(masked_keys[g, rows, :], queries)
            scores[rows, :] = block
            top = jnp.max(block, axis=0, keepdims=True)
            peak = top if peak is None else jnp.maximum(peak, top)
        total, out = None, None
        for b in range(KEYS // KEY_BLOCK):
            rows = slice(b * KEY_BLOCK, (b + 1) * KEY_BLOCK)
            exps = jnp.exp2((scores[rows, :] - peak) * TO_BASE_TWO)
            part = jnp.sum(exps, axis=0, keepdims=True)
            piece = dot_nn(values_t[g, :, rows], exps.astype(BF))
            total = part if total is None else total + part
            out = piece if out is None else out + piece
        put_two_heads(mixed_ref, pair, (out / total).T.astype(BF))
        spread_ref[pl.ds(pair, 1), :] = peak * TO_BASE_TWO + jnp.log2(total)
        return carry

    def row_copies(f):
        return [
            send(
                sent_rows.at[f, other], rows_in.at[f, me],
                row_send.at[f, d], row_recv.at[f, d], other,
            )
            for d, other in enumerate(others)
        ]

    def own_rows(f):
        return pltpu.make_async_copy(sent_rows.at[f, me], rows_in.at[f, me], row_own.at[f])

    def quarter(f, carry):
        lax.fori_loop(f * (PAIRS // FOLDS), (f + 1) * (PAIRS // FOLDS), step, 0)
        columns = mixed_ref[:, pl.ds(pl.multiple_of(f * WIDE, WIDE), WIDE)]
        picked = folded(dot_nn(mask, columns).astype(BF), swap)
        sent_rows[f] = picked.reshape(SLOTS, SLAB, WIDE // FOLDS)
        for copy in row_copies(f):
            copy.start()
        own_rows(f).start()
        return carry

    lax.fori_loop(0, FOLDS, quarter, 0)

    features = mixed_ref[...].astype(F32)
    factor = jnp.broadcast_to(rms_factor(features), (ROWS, 128))
    padded, _ = slot_mask(expert_ranks(ids_ref, trainable_ref), 16)
    picked = exact(jnp.where(padded, 1.0, 0.0), factor)
    sent_factors[...] = picked.reshape(SLOTS, 16, 128)
    factors = []
    for d, other in enumerate(others):
        copy = send(
            sent_factors.at[other], factors_in.at[me], factor_send.at[d], factor_recv.at[d], other
        )
        copy.start()
        factors.append(copy)
    own_factor = pltpu.make_async_copy(sent_factors.at[me], factors_in.at[me], own_sem.at[2])
    own_factor.start()

    for copy in slabs:
        copy.wait()
    own_slab.wait()
    for rows, a, values in unfolded(slabs_in[...].reshape(SLAB_ROWS, WIDE), swap):
        grads_ref[rows, a * WIDE : (a + 1) * WIDE] = values.astype(BF)

    narrow = WIDE // FOLDS

    def finish(f, carry):
        for copy in row_copies(f):
            copy.wait()
        own_rows(f).wait()
        for rows, a, values in unfolded(rows_in[f].reshape(SLAB_ROWS, narrow), swap):
            at = pl.multiple_of(f * WIDE + a * narrow, narrow)
            rows_ref[rows, pl.ds(at, narrow)] = values.astype(BF)
        return carry

    lax.fori_loop(0, FOLDS, finish, 0)
    for copy in factors:
        copy.wait()
    own_factor.wait()
    n = lax.broadcasted_iota(jnp.int32, (SLOTS * CAP, SLOTS * 16), 0)
    m = lax.broadcasted_iota(jnp.int32, (SLOTS * CAP, SLOTS * 16), 1)
    kept = jnp.where(m == n + (16 - CAP) * tenth(n), 1.0, 0.0)
    factor = exact(kept, factors_in[...].reshape(SLOTS * 16, 128))[:, :1]
    rows_ref[...] = (rows_ref[...].astype(F32) * factor * gain_ref[...]).astype(BF)


def expert_kernel(
    mine_ref, rows_ref, grads_ref, w_hbm_ref, terms_ref, products_ref, back_ref,
    routed_t, weighted_t, returned, w_ref, w_sem,
):
    loads = {}
    for step in range(2):
        for i in range(3):
            units = slice(step * (H // 2), (step + 1) * (H // 2))
            loads[step, i] = pltpu.make_async_copy(
                w_hbm_ref.at[i, units], w_ref.at[i, units], w_sem.at[step, i]
            )
            loads[step, i].start()
    routed_t[...] = rows_ref[...].T
    weighted_t[...] = grads_ref[...].T
    half = H // 2
    for step in range(2):
        units = slice(step * half, (step + 1) * half)
        loads[step, 0].wait()
        gate_in = dot_nn(w_ref[0, units, :], routed_t[...])
        loads[step, 1].wait()
        up_in = dot_nn(w_ref[1, units, :], routed_t[...])
        loads[step, 2].wait()
        back = dot_nn(w_ref[2, units, :], weighted_t[...])
        sigma = jax.nn.sigmoid(gate_in)
        activated = gate_in * sigma
        grad_gate = (back * up_in * sigma * (1.0 + gate_in * (1.0 - sigma))).astype(BF)
        grad_up = (back * activated).astype(BF)
        place = lax.rem(step + mine_ref[0], 2)
        products_ref[place] = (activated * up_in).astype(BF)
        for x in range(4):
            terms_ref[x, place, 0] = grad_gate[x * PART : (x + 1) * PART]
            terms_ref[x, place, 1] = grad_up[x * PART : (x + 1) * PART]
        grad_gate, grad_up = grad_gate.T, grad_up.T
        for f in range(FOLDS):
            at = slice(f * WIDE, (f + 1) * WIDE)
            part = dot_nn(grad_gate, w_ref[0, units, at]) + dot_nn(grad_up, w_ref[1, units, at])
            if step == 0:
                returned[:, at] = part
            else:
                returned[:, at] += part
    back_ref[...] = folded(returned[...].astype(BF), swap_mask())


def down_kernel(own_ref, other_ref, own_products_ref, other_products_ref, out_ref):
    out_ref[...] = (
        dot_nn(own_products_ref[0], own_ref[...])
        + dot_nn(other_products_ref[...], other_ref[...])
    ).astype(BF)


def gate_up_kernel(terms_ref, rows_ref, kept_ref, given_ref):
    total = None
    for k in range(4):
        left = terms_ref[k].reshape(4 * PART, SLOTS * CAP)
        part = dot_nn(left, rows_ref[k])
        total = part if total is None else total + part
    kept_ref[...] = total[: 2 * PART].astype(BF)
    given_ref[...] = total[2 * PART :].astype(BF)


def finish_kernel(kept_ref, taken_ref, down_ref, out_ref):
    for i in range(2):
        at = slice(i * PART, (i + 1) * PART)
        out_ref[i] = (kept_ref[at].astype(F32) + taken_ref[at].astype(F32)).astype(BF)
    out_ref[2] = down_ref[...]


def fill_keys(kv_ref, hidden_ref, g, masked_keys, keys_t, hides):
    keys = kv_ref[:, g * HEAD_SIZE : (g + 1) * HEAD_SIZE]
    masked_keys[:, :HEAD_SIZE] = keys
    masked_keys[:, HEAD_SIZE:] = hidden_ref[...]
    keys_t[...] = keys.T
    hides[...] = diagonal()


def backward_pairs(
    g, first, last, q_ref, kv_ref, mixed_ref, spread_ref, grad_mixed_ref, d_query_ref,
    masked_keys, keys_t, hides, key_sums, value_sums,
):
    at = (KEY_VALUE_HEADS + g) * HEAD_SIZE

    def step(pair, carry):
        plain = two_heads(q_ref, pair)
        queries = jnp.concatenate([plain, hides[...]], axis=1)
        grads = two_heads(grad_mixed_ref, pair)
        products = grads.astype(F32) * two_heads(mixed_ref, pair).astype(F32)
        delta = jnp.sum(products.T, axis=0, keepdims=True)
        spread = spread_ref[pl.ds(pair, 1), :]
        d_query = None
        for b in range(KEYS // KEY_BLOCK):
            rows = slice(b * KEY_BLOCK, (b + 1) * KEY_BLOCK)
            values = kv_ref[rows, at : at + HEAD_SIZE]
            raw = dot_nt(masked_keys[rows, :], queries)
            probs = jnp.exp2(raw * TO_BASE_TWO - spread)
            pushed = dot_nt(values, grads)
            slopes = (probs * (pushed - delta)).astype(BF)
            value_sums[rows, :] += dot_nn(probs.astype(BF), grads)
            key_sums[rows, :] += dot_nn(slopes, plain)
            piece = dot_nn(keys_t[:, rows], slopes)
            d_query = piece if d_query is None else d_query + piece
        put_two_heads(d_query_ref, pair, (d_query * INV_ROOT).T.astype(BF))
        return carry

    lax.fori_loop(first, last, step, 0)


def first_backward_kernel(
    q_ref, kv_ref, hidden_ref, ids_ref, trainable_ref, gain_ref,
    mixed_ref, spread_ref, up_ref, echo_ref,
    d_query_ref, d_kv_ref, grad_mixed_ref,
    masked_keys, keys_t, hides, key_sums, value_sums, echoed,
):
    mask, _ = slot_mask(expert_ranks(ids_ref, trainable_ref), CAP)
    mask = jnp.where(mask, 1.0, 0.0).astype(BF)
    for rows, a, values in unfolded(echo_ref[...], swap_mask()):
        echoed[rows, a * WIDE : (a + 1) * WIDE] = values.astype(BF)
    features = mixed_ref[...].astype(F32)
    factor = rms_factor(features)
    gradnorm = gain_ref[...] * dot_tn(mask, echoed[...])
    across = jnp.mean(gradnorm * features, axis=1, keepdims=True)
    grad_mixed_ref[...] = (
        up_ref[...].astype(F32)
        + factor * gradnorm
        - features * (factor * factor * factor) * across
    ).astype(BF)
    fill_keys(kv_ref, hidden_ref, 0, masked_keys, keys_t, hides)
    key_sums[...] = jnp.zeros_like(key_sums)
    value_sums[...] = jnp.zeros_like(value_sums)
    backward_pairs(
        0, 0, PAIRS // 2, q_ref, kv_ref, mixed_ref, spread_ref, grad_mixed_ref, d_query_ref,
        masked_keys, keys_t, hides, key_sums, value_sums,
    )
    d_kv_ref[:, :HEAD_SIZE] = (key_sums[...] * INV_ROOT).astype(BF)
    d_kv_ref[:, HEAD_SIZE:] = value_sums[...].astype(BF)


def greet(targets):
    barrier = pltpu.get_barrier_semaphore()
    for target in targets:
        pl.semaphore_signal(barrier, inc=1, device_id={"ctx": target}, device_id_type=MESH)
    pl.semaphore_wait(barrier, len(targets))


def send(source, target, send_sem, recv_sem, device):
    return pltpu.make_async_remote_copy(
        src_ref=source, dst_ref=target, send_sem=send_sem, recv_sem=recv_sem,
        device_id={"ctx": device}, device_id_type=MESH,
    )


def second_backward_kernel(
    q_ref, kv_ref, hidden_ref, mixed_ref, spread_ref, grad_mixed_ref, first_query_ref, first_kv_ref,
    d_query_ref, key_out_ref, value_out_ref,
    masked_keys, keys_t, hides, key_sums, value_sums,
    d_kv, near, sums, landed, near_send, near_recv, send_sem, recv_sem,
):
    me = lax.axis_index("ctx")
    chip, core = lax.div(me, 2), lax.rem(me, 2)
    sibling = 2 * chip + 1 - core
    chips = [lax.rem(chip + d, N_CHIP) for d in range(N_CHIP)]
    order = [*range(1, N_CHIP), 0]
    greet([*(2 * c + core for c in chips[1:]), sibling])

    def share(g, blocks):
        copies = {}
        for d in order:
            copies[d] = send(
                blocks.at[2 * chips[d] + 1 - core], near.at[g, d],
                near_send.at[g, d], near_recv.at[g, d], sibling,
            )
            copies[d].start()
        return copies

    def cross(g, blocks, shared):
        copies = []
        for d in order:
            shared[d].wait_recv()
            both = blocks[2 * chips[d] + core].astype(F32) + near[g, d].astype(F32)
            sums[g, d] = both.astype(BF)
            if d:
                copy = send(
                    sums.at[g, d], landed.at[g, d], send_sem.at[g, d], recv_sem.at[g, d],
                    2 * chips[d] + core,
                )
                copy.start()
                copies.append(copy)
        return copies

    def total(g, copies):
        result = sums[g, 0].astype(F32)
        for d, copy in enumerate(copies, start=1):
            copy.wait_recv()
            result = result + landed[g, d].astype(F32)
        at = slice(g * HEAD_SIZE, (g + 1) * HEAD_SIZE)
        key_out_ref[:, at] = result[:, :HEAD_SIZE].astype(BF)
        value_out_ref[:, at] = result[:, HEAD_SIZE:].astype(BF)

    def pairs(first, last):
        backward_pairs(
            1, first, last, q_ref, kv_ref, mixed_ref, spread_ref, grad_mixed_ref, d_query_ref,
            masked_keys, keys_t, hides, key_sums, value_sums,
        )

    shared_0 = share(0, first_kv_ref)
    d_query_ref[:, : D // 2] = first_query_ref[...]
    fill_keys(kv_ref, hidden_ref, 1, masked_keys, keys_t, hides)
    key_sums[...] = jnp.zeros_like(key_sums)
    value_sums[...] = jnp.zeros_like(value_sums)
    pairs(PAIRS // 2, PAIRS // 2 + 2)
    copies_0 = cross(0, first_kv_ref, shared_0)
    pairs(PAIRS // 2 + 2, PAIRS)
    d_kv[:, :, :HEAD_SIZE] = (
        (key_sums[...] * INV_ROOT).astype(BF).reshape(N_CTX, ROWS, HEAD_SIZE)
    )
    d_kv[:, :, HEAD_SIZE:] = value_sums[...].astype(BF).reshape(N_CTX, ROWS, HEAD_SIZE)
    shared_1 = share(1, d_kv)
    copies_1 = cross(1, d_kv, shared_1)
    total(0, copies_0)
    total(1, copies_1)
    for copy in copies_0 + copies_1:
        copy.wait_send()
    for d in order:
        shared_0[d].wait_send()
        shared_1[d].wait_send()


def return_kernel(
    x_ref, terms_ref, products_ref, out_ref, terms_out_ref, products_out_ref,
    send_sem, recv_sem, term_send, term_recv, pair_sem, own_sem,
):
    me, dp = lax.axis_index("ctx"), lax.axis_index("dp")
    x = lax.rem(dp, 4)
    others = [lax.rem(me + d, N_CTX) for d in range(1, N_CTX)]
    line = [lax.rem(x + k, 4) for k in range(1, 4)]
    pair = lax.rem(dp + 4, 8)
    barrier = pltpu.get_barrier_semaphore()
    for other in others:
        pl.semaphore_signal(barrier, inc=1, device_id={"ctx": other}, device_id_type=MESH)
    for other in [dp - x + k for k in line] + [pair]:
        pl.semaphore_signal(barrier, inc=1, device_id={"dp": other}, device_id_type=MESH)
    pl.semaphore_wait(barrier, N_CTX + 3)
    copies = []
    for d, other in enumerate(others):
        copies.append(
            send(x_ref.at[other], out_ref.at[me], send_sem.at[d], recv_sem.at[d], other)
        )
    for d, k in enumerate(line):
        copies.append(
            pltpu.make_async_remote_copy(
                src_ref=terms_ref.at[k], dst_ref=terms_out_ref.at[x],
                send_sem=term_send.at[d], recv_sem=term_recv.at[d],
                device_id={"dp": dp - x + k}, device_id_type=MESH,
            )
        )
    copies.append(
        pltpu.make_async_remote_copy(
            src_ref=products_ref.at[1], dst_ref=products_out_ref,
            send_sem=pair_sem.at[0], recv_sem=pair_sem.at[1],
            device_id={"dp": pair}, device_id_type=MESH,
        )
    )
    copies.append(pltpu.make_async_copy(x_ref.at[me], out_ref.at[me], own_sem.at[0]))
    copies.append(pltpu.make_async_copy(terms_ref.at[x], terms_out_ref.at[x], own_sem.at[1]))
    for copy in copies:
        copy.start()
    for copy in copies:
        copy.wait()


def dma(count):
    return pltpu.SemaphoreType.DMA((count,))


def over_pair(array):
    return lax.ppermute(array, "dp", [(i, (i + 4) % 8) for i in range(8)])


def per_device(
    query, key, value, span_order, expert_ids, expert_gates,
    trainable, norm_gain, upstream, expert_weights,
):
    bf_shape = lambda *s: jax.ShapeDtypeStruct(s, BF)
    half = ROWS // 2
    place = (span_order[0][:, None] * half + jnp.arange(half, dtype=jnp.int32)[None, :]).reshape(-1)
    own_place = lax.dynamic_slice_in_dim(place, lax.axis_index("ctx") * ROWS, ROWS)
    hidden = (place[:, None] > own_place[None, :]).astype(BF)
    ids, named = expert_ids[0].T, trainable[:, None]
    gain = norm_gain[None, :]
    weights = expert_weights[0].transpose(1, 0, 2)

    slab_shape = bf_shape(SLAB_ROWS, WIDE)
    sent_grads = pl.pallas_call(
        weighted_kernel, out_shape=slab_shape, in_specs=in_vmem(4), out_specs=in_vmem(1)[0],
        name="weighted", **local(10**9, 24),
    )(ids, expert_gates[0].T, named, upstream[0])

    groups = KEY_VALUE_HEADS
    slabs = (SLOTS, SLAB, WIDE)
    quarters = (FOLDS, SLOTS, SLAB, WIDE // FOLDS)
    whole, mixed, spread, rows, grads = pl.pallas_call(
        forward_kernel,
        out_shape=(
            bf_shape(N_CTX, ROWS, 2 * groups * HEAD_SIZE),
            bf_shape(ROWS, D),
            jax.ShapeDtypeStruct((PAIRS, 2 * ROWS), F32),
            bf_shape(SLOTS * CAP, D),
            bf_shape(SLOTS * CAP, D),
        ),
        in_specs=in_vmem(7),
        out_specs=tuple(in_vmem(5)),
        scratch_shapes=[
            pltpu.VMEM((groups, KEYS, 2 * HEAD_SIZE), BF),
            pltpu.VMEM((groups, HEAD_SIZE, KEYS), BF),
            pltpu.VMEM((2 * ROWS, ROWS), BF),
            pltpu.VMEM((KEYS, 2 * ROWS), F32),
            pltpu.VMEM(quarters, BF),
            pltpu.VMEM((SLOTS, 16, 128), F32),
            pltpu.VMEM(slabs, BF),
            pltpu.VMEM(quarters, BF),
            pltpu.VMEM((SLOTS, 16, 128), F32),
            dma(7), dma(7), dma(7), dma(7), dma(2), dma(3), dma(15), dma(15),
            pltpu.SemaphoreType.DMA((FOLDS, 15)), pltpu.SemaphoreType.DMA((FOLDS, 15)),
            dma(FOLDS), dma(15), dma(15),
        ],
        compiler_params=pltpu.CompilerParams(
            collective_id=0, has_side_effects=True, vmem_limit_bytes=36 * 2**20
        ),
        cost_estimate=pl.CostEstimate(flops=2 * 10**10, bytes_accessed=2**26, transcendentals=0),
        name="attention",
    )(
        jnp.concatenate([key[0], value[0]], axis=1), sent_grads.reshape(slabs),
        query[0], hidden, ids, named, gain,
    )
    whole = whole.reshape(KEYS, -1)
    other_grads = over_pair(grads)
    all_rows = lax.all_gather(rows, "dp", axis=0, axis_index_groups=X_GROUPS)

    mine = lax.div(lax.axis_index("dp"), 4)
    half, taken_rows = H // 2, SLOTS * CAP
    term_shape = (4, 2, 2, PART, taken_rows)
    terms, products, sent_back = pl.pallas_call(
        expert_kernel,
        out_shape=(bf_shape(*term_shape), bf_shape(2, half, taken_rows), slab_shape),
        in_specs=[
            pl.BlockSpec(memory_space=pltpu.SMEM),
            *in_vmem(2),
            pl.BlockSpec(memory_space=pl.ANY),
        ],
        out_specs=tuple(in_vmem(3)),
        scratch_shapes=[
            pltpu.VMEM((D, taken_rows), BF),
            pltpu.VMEM((D, taken_rows), BF),
            pltpu.VMEM((taken_rows, D), F32),
            pltpu.VMEM((3, H, D), BF),
            pltpu.SemaphoreType.DMA((2, 3)),
        ],
        name="experts",
        **local(10**10),
    )(mine[None], rows, grads, weights)

    echo, near_terms, other_products = pl.pallas_call(
        return_kernel,
        out_shape=(bf_shape(*slabs), bf_shape(*term_shape), bf_shape(half, taken_rows)),
        in_specs=in_vmem(3),
        out_specs=tuple(in_vmem(3)),
        scratch_shapes=[dma(15), dma(15), dma(3), dma(3), dma(2), dma(2)],
        compiler_params=pltpu.CompilerParams(
            collective_id=1, has_side_effects=True, vmem_limit_bytes=VMEM_LIMIT
        ),
        cost_estimate=pl.CostEstimate(flops=0, bytes_accessed=2**26, transcendentals=0),
        name="return",
    )(sent_back.reshape(slabs), terms, products)
    echo = echo.reshape(SLAB_ROWS, WIDE)

    across = lambda rows: pl.BlockSpec((rows, WIDE), lambda i: (0, i))
    fixed = lambda *shape: pl.BlockSpec(shape, lambda i: (0,) * len(shape))
    down = pl.pallas_call(
        down_kernel,
        grid=(FOLDS,),
        out_shape=bf_shape(half, D),
        in_specs=[
            across(taken_rows), across(taken_rows),
            pl.BlockSpec((1, half, taken_rows), lambda i: (0, 0, 0)), fixed(half, taken_rows),
        ],
        out_specs=across(half),
        name="down_terms",
        **local(4 * 10**9),
    )(grads, other_grads, products, other_products)
    down, all_rows, near_terms = lax.optimization_barrier((down, all_rows, near_terms))
    down = lax.psum_scatter(
        down, "dp", scatter_dimension=0, tiled=True, axis_index_groups=X_GROUPS
    )

    kept, given = pl.pallas_call(
        gate_up_kernel,
        grid=(FOLDS,),
        out_shape=(bf_shape(2 * PART, D), bf_shape(2 * PART, D)),
        in_specs=[
            fixed(*term_shape),
            pl.BlockSpec((4, taken_rows, WIDE), lambda i: (0, 0, i)),
        ],
        out_specs=(across(2 * PART), across(2 * PART)),
        name="gate_up_terms",
        **local(4 * 10**9),
    )(near_terms, all_rows)
    taken = over_pair(given)
    echo, kept = lax.optimization_barrier((echo, kept))
    kept_scratch = [
        pltpu.VMEM((KEYS, 2 * HEAD_SIZE), BF),
        pltpu.VMEM((HEAD_SIZE, KEYS), BF),
        pltpu.VMEM((2 * ROWS, ROWS), BF),
        pltpu.VMEM((KEYS, HEAD_SIZE), F32),
        pltpu.VMEM((KEYS, HEAD_SIZE), F32),
    ]
    first_query, first_kv, grad_mixed = pl.pallas_call(
        first_backward_kernel,
        out_shape=(bf_shape(ROWS, D // 2), bf_shape(KEYS, 2 * HEAD_SIZE), bf_shape(ROWS, D)),
        in_specs=in_vmem(10),
        out_specs=tuple(in_vmem(3)),
        scratch_shapes=[*kept_scratch, pltpu.VMEM((SLOTS * CAP, D), BF)],
        name="attention_grads_0",
        **local(2 * 10**10),
    )(query[0], whole, hidden, ids, named, gain, mixed, spread, upstream[0], echo)
    blocks = (N_CTX, ROWS, 2 * HEAD_SIZE)
    slots = pltpu.VMEM((groups, N_CHIP, ROWS, 2 * HEAD_SIZE), BF)
    dmas = pltpu.SemaphoreType.DMA((groups, N_CHIP))
    d_query, d_key, d_value = pl.pallas_call(
        second_backward_kernel,
        out_shape=(bf_shape(ROWS, D), *[bf_shape(ROWS, groups * HEAD_SIZE)] * 2),
        in_specs=in_vmem(8),
        out_specs=tuple(in_vmem(3)),
        scratch_shapes=[
            *kept_scratch, pltpu.VMEM(blocks, BF), slots, slots, slots, dmas, dmas, dmas, dmas,
        ],
        compiler_params=pltpu.CompilerParams(
            collective_id=2, has_side_effects=True, vmem_limit_bytes=VMEM_LIMIT
        ),
        cost_estimate=pl.CostEstimate(flops=2 * 10**10, bytes_accessed=2**26, transcendentals=0),
        name="attention_grads_1",
    )(
        query[0], whole, hidden, mixed, spread, grad_mixed, first_query, first_kv.reshape(blocks)
    )
    expert_grads = pl.pallas_call(
        finish_kernel, out_shape=bf_shape(3, PART, D), in_specs=in_vmem(3),
        out_specs=in_vmem(1)[0], name="expert_grads", **local(10**7),
    )(kept, taken, down)
    return (
        d_query[None],
        d_key[None],
        d_value[None],
        expert_grads.transpose(1, 0, 2)[None],
    )


def solution(mesh):
    in_specs = (
        P("dp", "ctx", None),
        P("dp", "ctx", None),
        P("dp", "ctx", None),
        P("dp", None),
        P("dp", "ctx", None),
        P("dp", "ctx", None),
        P(),
        P(),
        P("dp", "ctx", None),
        P("ctx", None, None, None),
    )
    out_specs = (
        P("dp", "ctx", None),
        P("dp", "ctx", None),
        P("dp", "ctx", None),
        P("ctx", "dp", None, None),
    )
    return jax.shard_map(
        per_device, mesh=mesh, in_specs=in_specs, out_specs=out_specs, check_vma=False
    )
```

```python
import math

import jax
import jax.numpy as jnp
from jax import lax
from jax.experimental import pallas as pl
from jax.experimental.pallas import tpu as pltpu
from jax.sharding import PartitionSpec as P

D = 4096
QUERY_HEADS = 32
KEY_VALUE_HEADS = 2
HEAD_SIZE = 128
TOP = 8
CAP = 12
H = 768
N_CTX = 16
N_CHIP = 8
ROWS = 128
KEYS = 2048
SLOTS = 16
FOLDS = 4
WIDE = D // FOLDS
SLAB = CAP * FOLDS
SLAB_ROWS = SLOTS * SLAB
PAIRS = QUERY_HEADS // 2
KEY_BLOCK = 512
PART = H // 8

MASK_FILLER = -1e30
EPSILON = 1e-06
INV_ROOT = HEAD_SIZE ** (-0.5)
TO_BASE_TWO = INV_ROOT * math.log2(math.e)

X_GROUPS = [[0, 1, 2, 3], [4, 5, 6, 7]]
MESH = pl.DeviceIdType.MESH
VMEM_LIMIT = 40 * 2**20
BF = jnp.bfloat16
F32 = jnp.float32


def dot_nn(a, b):
    return lax.dot_general(a, b, (((1,), (0,)), ((), ())), preferred_element_type=F32)


def dot_nt(a, b):
    return lax.dot_general(a, b, (((1,), (1,)), ((), ())), preferred_element_type=F32)


def dot_tn(a, b):
    return lax.dot_general(a, b, (((0,), (0,)), ((), ())), preferred_element_type=F32)


def in_vmem(count):
    return [pl.BlockSpec(memory_space=pltpu.VMEM)] * count


def local(cost, limit=40):
    return dict(
        compiler_params=pltpu.CompilerParams(vmem_limit_bytes=limit * 2**20),
        cost_estimate=pl.CostEstimate(flops=cost, bytes_accessed=2**22, transcendentals=0),
    )


def expert_ranks(ids_ref, trainable_ref):
    hits = jnp.zeros((SLOTS, ROWS), F32)
    for k in range(TOP):
        hits = hits + jnp.where(ids_ref[k : k + 1, :] == trainable_ref[...], 1.0, 0.0)
    before = lax.broadcasted_iota(jnp.int32, (ROWS, ROWS), 0) < lax.broadcasted_iota(
        jnp.int32, (ROWS, ROWS), 1
    )
    rank = dot_nn(hits.astype(BF), jnp.where(before, 1.0, 0.0).astype(BF))
    return jnp.where(hits > 0.5, rank, -1.0)


def tenth(n):
    return lax.shift_right_logical(n * 5462, 16)


def slot_mask(rank, pad):
    rows = SLOTS * pad
    n = lax.broadcasted_iota(jnp.int32, (rows, SLOTS), 0)
    j = lax.broadcasted_iota(jnp.int32, (rows, SLOTS), 1)
    owner = tenth(n) if pad == CAP else lax.shift_right_logical(n, 4)
    spread = dot_nn(jnp.where(owner == j, 1.0, 0.0).astype(BF), rank.astype(BF))
    slot = n[:, :1] - pad * owner[:, :1]
    return spread == slot.astype(F32), owner


def swap_mask():
    o = lax.broadcasted_iota(jnp.int32, (4 * SLAB, 4 * SLAB), 0)
    i = lax.broadcasted_iota(jnp.int32, (4 * SLAB, 4 * SLAB), 1)
    a = sum(jnp.where(o >= SLAB * k, 1, 0) for k in range(1, 4))
    o = o - SLAB * a
    b = sum(jnp.where(o >= CAP * k, 1, 0) for k in range(1, 4))
    return jnp.where(i == SLAB * b + CAP * a + o - CAP * b, 1.0, 0.0).astype(BF)


def unfolded(slabs, swap):
    for g in range(4):
        rows = dot_nn(swap, slabs[g * 4 * SLAB : (g + 1) * 4 * SLAB])
        for a in range(FOLDS):
            yield slice(g * SLAB, (g + 1) * SLAB), a, rows[a * SLAB : (a + 1) * SLAB]


def folded(rows, swap):
    wide = rows.shape[1] // FOLDS
    slabs = []
    for g in range(4):
        at = slice(g * SLAB, (g + 1) * SLAB)
        pile = [rows[at, a * wide : (a + 1) * wide] for a in range(FOLDS)]
        slabs.append(dot_nn(swap, jnp.concatenate(pile, axis=0)).astype(BF))
    return jnp.concatenate(slabs, axis=0)


def exact(a, b):
    return lax.dot_general(
        a, b, (((1,), (0,)), ((), ())),
        precision=lax.Precision.HIGHEST, preferred_element_type=F32,
    )


def weighted_kernel(ids_ref, gates_ref, trainable_ref, up_ref, out_ref):
    rank = expert_ranks(ids_ref, trainable_ref)
    mask, owner = slot_mask(rank, CAP)
    gates = jnp.zeros((SLOTS, ROWS), F32)
    for k in range(TOP):
        same = ids_ref[k : k + 1, :] == trainable_ref[...]
        gates = gates + jnp.where(same, gates_ref[k : k + 1, :], 0.0)
    own = owner == lax.broadcasted_iota(jnp.int32, owner.shape, 1)
    gates = exact(jnp.where(own, 1.0, 0.0), gates)
    gate = jnp.sum(jnp.where(mask, gates, 0.0), axis=1, keepdims=True)
    rows = dot_nn(jnp.where(mask, 1.0, 0.0).astype(BF), up_ref[...])
    out_ref[...] = folded((gate * rows).astype(BF), swap_mask())


def two_heads(ref, pair):
    at = pl.multiple_of(pair * 2 * HEAD_SIZE, 2 * HEAD_SIZE)
    both = ref[:, pl.ds(at, 2 * HEAD_SIZE)]
    return jnp.concatenate([both[:, :HEAD_SIZE], both[:, HEAD_SIZE:]], axis=0)


def put_two_heads(ref, pair, stacked):
    at = pl.multiple_of(pair * 2 * HEAD_SIZE, 2 * HEAD_SIZE)
    ref[:, pl.ds(at, 2 * HEAD_SIZE)] = jnp.concatenate([stacked[:ROWS], stacked[ROWS:]], axis=1)


def diagonal():
    eye = lax.broadcasted_iota(jnp.int32, (ROWS, ROWS), 0) == lax.broadcasted_iota(
        jnp.int32, (ROWS, ROWS), 1
    )
    one = jnp.where(eye, MASK_FILLER, 0.0).astype(BF)
    return jnp.concatenate([one, one], axis=0)


def rms_factor(features):
    return lax.rsqrt(jnp.mean(features * features, axis=1, keepdims=True) + EPSILON)


def forward_kernel(
    kv_ref, slabs_ref, q_ref, hidden_ref, ids_ref, trainable_ref, gain_ref,
    whole_ref, mixed_ref, spread_ref, rows_ref, grads_ref,
    masked_keys, values_t, hides, scores, sent_rows, sent_factors, slabs_in, rows_in, factors_in,
    send_sem, recv_sem, pass_sem, passed_sem, near_sem, own_sem,
    slab_send, slab_recv, row_send, row_recv, row_own, factor_send, factor_recv,
):
    me = lax.axis_index("ctx")
    chip, core = lax.div(me, 2), lax.rem(me, 2)
    sibling = 2 * chip + 1 - core
    far = [2 * lax.rem(chip + d, N_CHIP) + core for d in range(1, N_CHIP)]
    others = [lax.rem(me + d, N_CTX) for d in range(1, N_CTX)]
    greet(others)
    copies = []
    for d, other in enumerate(far):
        copy = send(kv_ref, whole_ref.at[me], send_sem.at[d], recv_sem.at[d], other)
        copy.start()
        copies.append(copy)
    near = send(kv_ref, whole_ref.at[me], near_sem.at[0], near_sem.at[1], sibling)
    near.start()
    own = pltpu.make_async_copy(kv_ref, whole_ref.at[me], own_sem.at[0])
    own.start()

    slabs = []
    for d, other in enumerate(others):
        copy = send(
            slabs_ref.at[other], slabs_in.at[me], slab_send.at[d], slab_recv.at[d], other
        )
        copy.start()
        slabs.append(copy)
    own_slab = pltpu.make_async_copy(slabs_ref.at[me], slabs_in.at[me], own_sem.at[1])
    own_slab.start()

    mask, _ = slot_mask(expert_ranks(ids_ref, trainable_ref), CAP)
    mask = jnp.where(mask, 1.0, 0.0).astype(BF)
    swap = swap_mask()
    hides[...] = diagonal()
    for g in range(KEY_VALUE_HEADS):
        masked_keys[g, :, HEAD_SIZE:] = hidden_ref[...]

    passed = []
    for d in range(1, N_CHIP):
        source = 2 * lax.rem(chip + N_CHIP - d, N_CHIP) + core
        copies[d - 1].wait_recv()
        copy = send(
            whole_ref.at[source], whole_ref.at[source],
            pass_sem.at[d - 1], passed_sem.at[d - 1], sibling,
        )
        copy.start()
        passed.append(copy)
    for copy in copies:
        copy.wait_send()
    near.wait()
    own.wait()
    for copy in passed:
        copy.wait()

    for g in range(KEY_VALUE_HEADS):
        at = g * HEAD_SIZE
        keys = whole_ref[:, :, at : at + HEAD_SIZE].reshape(KEYS, HEAD_SIZE)
        masked_keys[g, :, :HEAD_SIZE] = keys
        at = (KEY_VALUE_HEADS + g) * HEAD_SIZE
        values_t[g] = whole_ref[:, :, at : at + HEAD_SIZE].reshape(KEYS, HEAD_SIZE).T

    def step(pair, carry):
        g = lax.div(pair, PAIRS // KEY_VALUE_HEADS)
        queries = jnp.concatenate([two_heads(q_ref, pair), hides[...]], axis=1)
        peak = None
        for b in range(KEYS // KEY_BLOCK):
            rows = slice(b * KEY_BLOCK, (b + 1) * KEY_BLOCK)
            block = dot_nt(masked_keys[g, rows, :], queries)
            scores[rows, :] = block
            top = jnp.max(block, axis=0, keepdims=True)
            peak = top if peak is None else jnp.maximum(peak, top)
        total, out = None, None
        for b in range(KEYS // KEY_BLOCK):
            rows = slice(b * KEY_BLOCK, (b + 1) * KEY_BLOCK)
            exps = jnp.exp2((scores[rows, :] - peak) * TO_BASE_TWO)
            part = jnp.sum(exps, axis=0, keepdims=True)
            piece = dot_nn(values_t[g, :, rows], exps.astype(BF))
            total = part if total is None else total + part
            out = piece if out is None else out + piece
        put_two_heads(mixed_ref, pair, (out / total).T.astype(BF))
        spread_ref[pl.ds(pair, 1), :] = peak * TO_BASE_TWO + jnp.log2(total)
        return carry

    def row_copies(f):
        return [
            send(
                sent_rows.at[f, other], rows_in.at[f, me],
                row_send.at[f, d], row_recv.at[f, d], other,
            )
            for d, other in enumerate(others)
        ]

    def own_rows(f):
        return pltpu.make_async_copy(sent_rows.at[f, me], rows_in.at[f, me], row_own.at[f])

    def quarter(f, carry):
        lax.fori_loop(f * (PAIRS // FOLDS), (f + 1) * (PAIRS // FOLDS), step, 0)
        columns = mixed_ref[:, pl.ds(pl.multiple_of(f * WIDE, WIDE), WIDE)]
        picked = folded(dot_nn(mask, columns).astype(BF), swap)
        sent_rows[f] = picked.reshape(SLOTS, SLAB, WIDE // FOLDS)
        for copy in row_copies(f):
            copy.start()
        own_rows(f).start()
        return carry

    lax.fori_loop(0, FOLDS, quarter, 0)

    features = mixed_ref[...].astype(F32)
    factor = jnp.broadcast_to(rms_factor(features), (ROWS, 128))
    padded, _ = slot_mask(expert_ranks(ids_ref, trainable_ref), 16)
    picked = exact(jnp.where(padded, 1.0, 0.0), factor)
    sent_factors[...] = picked.reshape(SLOTS, 16, 128)
    factors = []
    for d, other in enumerate(others):
        copy = send(
            sent_factors.at[other], factors_in.at[me], factor_send.at[d], factor_recv.at[d], other
        )
        copy.start()
        factors.append(copy)
    own_factor = pltpu.make_async_copy(sent_factors.at[me], factors_in.at[me], own_sem.at[2])
    own_factor.start()

    for copy in slabs:
        copy.wait()
    own_slab.wait()
    for rows, a, values in unfolded(slabs_in[...].reshape(SLAB_ROWS, WIDE), swap):
        grads_ref[rows, a * WIDE : (a + 1) * WIDE] = values.astype(BF)

    narrow = WIDE // FOLDS

    def finish(f, carry):
        for copy in row_copies(f):
            copy.wait()
        own_rows(f).wait()
        for rows, a, values in unfolded(rows_in[f].reshape(SLAB_ROWS, narrow), swap):
            at = pl.multiple_of(f * WIDE + a * narrow, narrow)
            rows_ref[rows, pl.ds(at, narrow)] = values.astype(BF)
        return carry

    lax.fori_loop(0, FOLDS, finish, 0)
    for copy in factors:
        copy.wait()
    own_factor.wait()
    n = lax.broadcasted_iota(jnp.int32, (SLOTS * CAP, SLOTS * 16), 0)
    m = lax.broadcasted_iota(jnp.int32, (SLOTS * CAP, SLOTS * 16), 1)
    kept = jnp.where(m == n + (16 - CAP) * tenth(n), 1.0, 0.0)
    factor = exact(kept, factors_in[...].reshape(SLOTS * 16, 128))[:, :1]
    rows_ref[...] = (rows_ref[...].astype(F32) * factor * gain_ref[...]).astype(BF)


def expert_kernel(
    mine_ref, rows_ref, grads_ref, w_hbm_ref, terms_ref, products_ref, back_ref,
    routed_t, weighted_t, returned, w_ref, w_sem,
):
    loads = {}
    for step in range(2):
        for i in range(3):
            units = slice(step * (H // 2), (step + 1) * (H // 2))
            loads[step, i] = pltpu.make_async_copy(
                w_hbm_ref.at[i, units], w_ref.at[i, units], w_sem.at[step, i]
            )
            loads[step, i].start()
    routed_t[...] = rows_ref[...].T
    weighted_t[...] = grads_ref[...].T
    half = H // 2
    for step in range(2):
        units = slice(step * half, (step + 1) * half)
        loads[step, 0].wait()
        gate_in = dot_nn(w_ref[0, units, :], routed_t[...])
        loads[step, 1].wait()
        up_in = dot_nn(w_ref[1, units, :], routed_t[...])
        loads[step, 2].wait()
        back = dot_nn(w_ref[2, units, :], weighted_t[...])
        sigma = jax.nn.sigmoid(gate_in)
        activated = gate_in * sigma
        grad_gate = (back * up_in * sigma * (1.0 + gate_in * (1.0 - sigma))).astype(BF)
        grad_up = (back * activated).astype(BF)
        place = lax.rem(step + mine_ref[0], 2)
        products_ref[place] = (activated * up_in).astype(BF)
        for x in range(4):
            terms_ref[x, place, 0] = grad_gate[x * PART : (x + 1) * PART]
            terms_ref[x, place, 1] = grad_up[x * PART : (x + 1) * PART]
        grad_gate, grad_up = grad_gate.T, grad_up.T
        for f in range(FOLDS):
            at = slice(f * WIDE, (f + 1) * WIDE)
            part = dot_nn(grad_gate, w_ref[0, units, at]) + dot_nn(grad_up, w_ref[1, units, at])
            if step == 0:
                returned[:, at] = part
            else:
                returned[:, at] += part
    back_ref[...] = folded(returned[...].astype(BF), swap_mask())


def down_kernel(own_ref, other_ref, own_products_ref, other_products_ref, out_ref):
    out_ref[...] = (
        dot_nn(own_products_ref[0], own_ref[...])
        + dot_nn(other_products_ref[...], other_ref[...])
    ).astype(BF)


def gate_up_kernel(terms_ref, rows_ref, kept_ref, given_ref):
    total = None
    for k in range(4):
        left = terms_ref[k].reshape(4 * PART, SLOTS * CAP)
        part = dot_nn(left, rows_ref[k])
        total = part if total is None else total + part
    kept_ref[...] = total[: 2 * PART].astype(BF)
    given_ref[...] = total[2 * PART :].astype(BF)


def finish_kernel(kept_ref, taken_ref, down_ref, out_ref):
    for i in range(2):
        at = slice(i * PART, (i + 1) * PART)
        out_ref[i] = (kept_ref[at].astype(F32) + taken_ref[at].astype(F32)).astype(BF)
    out_ref[2] = down_ref[...]


def fill_keys(kv_ref, hidden_ref, g, masked_keys, keys_t, hides):
    keys = kv_ref[:, g * HEAD_SIZE : (g + 1) * HEAD_SIZE]
    masked_keys[:, :HEAD_SIZE] = keys
    masked_keys[:, HEAD_SIZE:] = hidden_ref[...]
    keys_t[...] = keys.T
    hides[...] = diagonal()


def backward_pairs(
    g, first, last, q_ref, kv_ref, mixed_ref, spread_ref, grad_mixed_ref, d_query_ref,
    masked_keys, keys_t, hides, key_sums, value_sums,
):
    at = (KEY_VALUE_HEADS + g) * HEAD_SIZE

    def step(pair, carry):
        plain = two_heads(q_ref, pair)
        queries = jnp.concatenate([plain, hides[...]], axis=1)
        grads = two_heads(grad_mixed_ref, pair)
        products = grads.astype(F32) * two_heads(mixed_ref, pair).astype(F32)
        delta = jnp.sum(products.T, axis=0, keepdims=True)
        spread = spread_ref[pl.ds(pair, 1), :]
        d_query = None
        for b in range(KEYS // KEY_BLOCK):
            rows = slice(b * KEY_BLOCK, (b + 1) * KEY_BLOCK)
            values = kv_ref[rows, at : at + HEAD_SIZE]
            raw = dot_nt(masked_keys[rows, :], queries)
            probs = jnp.exp2(raw * TO_BASE_TWO - spread)
            pushed = dot_nt(values, grads)
            slopes = (probs * (pushed - delta)).astype(BF)
            value_sums[rows, :] += dot_nn(probs.astype(BF), grads)
            key_sums[rows, :] += dot_nn(slopes, plain)
            piece = dot_nn(keys_t[:, rows], slopes)
            d_query = piece if d_query is None else d_query + piece
        put_two_heads(d_query_ref, pair, (d_query * INV_ROOT).T.astype(BF))
        return carry

    lax.fori_loop(first, last, step, 0)


def first_backward_kernel(
    q_ref, kv_ref, hidden_ref, ids_ref, trainable_ref, gain_ref,
    mixed_ref, spread_ref, up_ref, echo_ref,
    d_query_ref, d_kv_ref, grad_mixed_ref,
    masked_keys, keys_t, hides, key_sums, value_sums, echoed,
):
    mask, _ = slot_mask(expert_ranks(ids_ref, trainable_ref), CAP)
    mask = jnp.where(mask, 1.0, 0.0).astype(BF)
    for rows, a, values in unfolded(echo_ref[...], swap_mask()):
        echoed[rows, a * WIDE : (a + 1) * WIDE] = values.astype(BF)
    features = mixed_ref[...].astype(F32)
    factor = rms_factor(features)
    gradnorm = gain_ref[...] * dot_tn(mask, echoed[...])
    across = jnp.mean(gradnorm * features, axis=1, keepdims=True)
    grad_mixed_ref[...] = (
        up_ref[...].astype(F32)
        + factor * gradnorm
        - features * (factor * factor * factor) * across
    ).astype(BF)
    fill_keys(kv_ref, hidden_ref, 0, masked_keys, keys_t, hides)
    key_sums[...] = jnp.zeros_like(key_sums)
    value_sums[...] = jnp.zeros_like(value_sums)
    backward_pairs(
        0, 0, PAIRS // 2, q_ref, kv_ref, mixed_ref, spread_ref, grad_mixed_ref, d_query_ref,
        masked_keys, keys_t, hides, key_sums, value_sums,
    )
    d_kv_ref[:, :HEAD_SIZE] = (key_sums[...] * INV_ROOT).astype(BF)
    d_kv_ref[:, HEAD_SIZE:] = value_sums[...].astype(BF)


def greet(targets):
    barrier = pltpu.get_barrier_semaphore()
    for target in targets:
        pl.semaphore_signal(barrier, inc=1, device_id={"ctx": target}, device_id_type=MESH)
    pl.semaphore_wait(barrier, len(targets))


def send(source, target, send_sem, recv_sem, device):
    return pltpu.make_async_remote_copy(
        src_ref=source, dst_ref=target, send_sem=send_sem, recv_sem=recv_sem,
        device_id={"ctx": device}, device_id_type=MESH,
    )


def second_backward_kernel(
    q_ref, kv_ref, hidden_ref, mixed_ref, spread_ref, grad_mixed_ref, first_query_ref, first_kv_ref,
    d_query_ref, key_out_ref, value_out_ref,
    masked_keys, keys_t, hides, key_sums, value_sums,
    d_kv, near, sums, landed, near_send, near_recv, send_sem, recv_sem,
):
    me = lax.axis_index("ctx")
    chip, core = lax.div(me, 2), lax.rem(me, 2)
    sibling = 2 * chip + 1 - core
    chips = [lax.rem(chip + d, N_CHIP) for d in range(N_CHIP)]
    order = [*range(1, N_CHIP), 0]
    greet([*(2 * c + core for c in chips[1:]), sibling])

    def share(g, blocks):
        copies = {}
        for d in order:
            copies[d] = send(
                blocks.at[2 * chips[d] + 1 - core], near.at[g, d],
                near_send.at[g, d], near_recv.at[g, d], sibling,
            )
            copies[d].start()
        return copies

    def cross(g, blocks, shared):
        copies = []
        for d in order:
            shared[d].wait_recv()
            both = blocks[2 * chips[d] + core].astype(F32) + near[g, d].astype(F32)
            sums[g, d] = both.astype(BF)
            if d:
                copy = send(
                    sums.at[g, d], landed.at[g, d], send_sem.at[g, d], recv_sem.at[g, d],
                    2 * chips[d] + core,
                )
                copy.start()
                copies.append(copy)
        return copies

    def total(g, copies):
        result = sums[g, 0].astype(F32)
        for d, copy in enumerate(copies, start=1):
            copy.wait_recv()
            result = result + landed[g, d].astype(F32)
        at = slice(g * HEAD_SIZE, (g + 1) * HEAD_SIZE)
        key_out_ref[:, at] = result[:, :HEAD_SIZE].astype(BF)
        value_out_ref[:, at] = result[:, HEAD_SIZE:].astype(BF)

    def pairs(first, last):
        backward_pairs(
            1, first, last, q_ref, kv_ref, mixed_ref, spread_ref, grad_mixed_ref, d_query_ref,
            masked_keys, keys_t, hides, key_sums, value_sums,
        )

    shared_0 = share(0, first_kv_ref)
    d_query_ref[:, : D // 2] = first_query_ref[...]
    fill_keys(kv_ref, hidden_ref, 1, masked_keys, keys_t, hides)
    key_sums[...] = jnp.zeros_like(key_sums)
    value_sums[...] = jnp.zeros_like(value_sums)
    pairs(PAIRS // 2, PAIRS // 2 + 2)
    copies_0 = cross(0, first_kv_ref, shared_0)
    pairs(PAIRS // 2 + 2, PAIRS)
    d_kv[:, :, :HEAD_SIZE] = (
        (key_sums[...] * INV_ROOT).astype(BF).reshape(N_CTX, ROWS, HEAD_SIZE)
    )
    d_kv[:, :, HEAD_SIZE:] = value_sums[...].astype(BF).reshape(N_CTX, ROWS, HEAD_SIZE)
    shared_1 = share(1, d_kv)
    copies_1 = cross(1, d_kv, shared_1)
    total(0, copies_0)
    total(1, copies_1)
    for copy in copies_0 + copies_1:
        copy.wait_send()
    for d in order:
        shared_0[d].wait_send()
        shared_1[d].wait_send()


def return_kernel(
    x_ref, terms_ref, products_ref, out_ref, terms_out_ref, products_out_ref,
    send_sem, recv_sem, term_send, term_recv, pair_sem, own_sem,
):
    me, dp = lax.axis_index("ctx"), lax.axis_index("dp")
    x = lax.rem(dp, 4)
    others = [lax.rem(me + d, N_CTX) for d in range(1, N_CTX)]
    line = [lax.rem(x + k, 4) for k in range(1, 4)]
    pair = lax.rem(dp + 4, 8)
    barrier = pltpu.get_barrier_semaphore()
    for other in others:
        pl.semaphore_signal(barrier, inc=1, device_id={"ctx": other}, device_id_type=MESH)
    for other in [dp - x + k for k in line] + [pair]:
        pl.semaphore_signal(barrier, inc=1, device_id={"dp": other}, device_id_type=MESH)
    pl.semaphore_wait(barrier, N_CTX + 3)
    copies = []
    for d, other in enumerate(others):
        copies.append(
            send(x_ref.at[other], out_ref.at[me], send_sem.at[d], recv_sem.at[d], other)
        )
    for d, k in enumerate(line):
        copies.append(
            pltpu.make_async_remote_copy(
                src_ref=terms_ref.at[k], dst_ref=terms_out_ref.at[x],
                send_sem=term_send.at[d], recv_sem=term_recv.at[d],
                device_id={"dp": dp - x + k}, device_id_type=MESH,
            )
        )
    copies.append(
        pltpu.make_async_remote_copy(
            src_ref=products_ref.at[1], dst_ref=products_out_ref,
            send_sem=pair_sem.at[0], recv_sem=pair_sem.at[1],
            device_id={"dp": pair}, device_id_type=MESH,
        )
    )
    copies.append(pltpu.make_async_copy(x_ref.at[me], out_ref.at[me], own_sem.at[0]))
    copies.append(pltpu.make_async_copy(terms_ref.at[x], terms_out_ref.at[x], own_sem.at[1]))
    for copy in copies:
        copy.start()
    for copy in copies:
        copy.wait()


def dma(count):
    return pltpu.SemaphoreType.DMA((count,))


def over_pair(array):
    return lax.ppermute(array, "dp", [(i, (i + 4) % 8) for i in range(8)])


def per_device(
    query, key, value, span_order, expert_ids, expert_gates,
    trainable, norm_gain, upstream, expert_weights,
):
    bf_shape = lambda *s: jax.ShapeDtypeStruct(s, BF)
    half = ROWS // 2
    place = (span_order[0][:, None] * half + jnp.arange(half, dtype=jnp.int32)[None, :]).reshape(-1)
    own_place = lax.dynamic_slice_in_dim(place, lax.axis_index("ctx") * ROWS, ROWS)
    hidden = (place[:, None] > own_place[None, :]).astype(BF)
    ids, named = expert_ids[0].T, trainable[:, None]
    gain = norm_gain[None, :]
    weights = expert_weights[0].transpose(1, 0, 2)

    slab_shape = bf_shape(SLAB_ROWS, WIDE)
    sent_grads = pl.pallas_call(
        weighted_kernel, out_shape=slab_shape, in_specs=in_vmem(4), out_specs=in_vmem(1)[0],
        name="weighted", **local(10**9, 24),
    )(ids, expert_gates[0].T, named, upstream[0])

    groups = KEY_VALUE_HEADS
    slabs = (SLOTS, SLAB, WIDE)
    quarters = (FOLDS, SLOTS, SLAB, WIDE // FOLDS)
    whole, mixed, spread, rows, grads = pl.pallas_call(
        forward_kernel,
        out_shape=(
            bf_shape(N_CTX, ROWS, 2 * groups * HEAD_SIZE),
            bf_shape(ROWS, D),
            jax.ShapeDtypeStruct((PAIRS, 2 * ROWS), F32),
            bf_shape(SLOTS * CAP, D),
            bf_shape(SLOTS * CAP, D),
        ),
        in_specs=in_vmem(7),
        out_specs=tuple(in_vmem(5)),
        scratch_shapes=[
            pltpu.VMEM((groups, KEYS, 2 * HEAD_SIZE), BF),
            pltpu.VMEM((groups, HEAD_SIZE, KEYS), BF),
            pltpu.VMEM((2 * ROWS, ROWS), BF),
            pltpu.VMEM((KEYS, 2 * ROWS), F32),
            pltpu.VMEM(quarters, BF),
            pltpu.VMEM((SLOTS, 16, 128), F32),
            pltpu.VMEM(slabs, BF),
            pltpu.VMEM(quarters, BF),
            pltpu.VMEM((SLOTS, 16, 128), F32),
            dma(7), dma(7), dma(7), dma(7), dma(2), dma(3), dma(15), dma(15),
            pltpu.SemaphoreType.DMA((FOLDS, 15)), pltpu.SemaphoreType.DMA((FOLDS, 15)),
            dma(FOLDS), dma(15), dma(15),
        ],
        compiler_params=pltpu.CompilerParams(
            collective_id=0, has_side_effects=True, vmem_limit_bytes=36 * 2**20
        ),
        cost_estimate=pl.CostEstimate(flops=2 * 10**10, bytes_accessed=2**26, transcendentals=0),
        name="attention",
    )(
        jnp.concatenate([key[0], value[0]], axis=1), sent_grads.reshape(slabs),
        query[0], hidden, ids, named, gain,
    )
    whole = whole.reshape(KEYS, -1)
    other_grads = over_pair(grads)
    all_rows = lax.all_gather(rows, "dp", axis=0, axis_index_groups=X_GROUPS)

    mine = lax.div(lax.axis_index("dp"), 4)
    half, taken_rows = H // 2, SLOTS * CAP
    term_shape = (4, 2, 2, PART, taken_rows)
    terms, products, sent_back = pl.pallas_call(
        expert_kernel,
        out_shape=(bf_shape(*term_shape), bf_shape(2, half, taken_rows), slab_shape),
        in_specs=[
            pl.BlockSpec(memory_space=pltpu.SMEM),
            *in_vmem(2),
            pl.BlockSpec(memory_space=pl.ANY),
        ],
        out_specs=tuple(in_vmem(3)),
        scratch_shapes=[
            pltpu.VMEM((D, taken_rows), BF),
            pltpu.VMEM((D, taken_rows), BF),
            pltpu.VMEM((taken_rows, D), F32),
            pltpu.VMEM((3, H, D), BF),
            pltpu.SemaphoreType.DMA((2, 3)),
        ],
        name="experts",
        **local(10**10),
    )(mine[None], rows, grads, weights)

    echo, near_terms, other_products = pl.pallas_call(
        return_kernel,
        out_shape=(bf_shape(*slabs), bf_shape(*term_shape), bf_shape(half, taken_rows)),
        in_specs=in_vmem(3),
        out_specs=tuple(in_vmem(3)),
        scratch_shapes=[dma(15), dma(15), dma(3), dma(3), dma(2), dma(2)],
        compiler_params=pltpu.CompilerParams(
            collective_id=1, has_side_effects=True, vmem_limit_bytes=VMEM_LIMIT
        ),
        cost_estimate=pl.CostEstimate(flops=0, bytes_accessed=2**26, transcendentals=0),
        name="return",
    )(sent_back.reshape(slabs), terms, products)
    echo = echo.reshape(SLAB_ROWS, WIDE)

    across = lambda rows: pl.BlockSpec((rows, WIDE), lambda i: (0, i))
    fixed = lambda *shape: pl.BlockSpec(shape, lambda i: (0,) * len(shape))
    down = pl.pallas_call(
        down_kernel,
        grid=(FOLDS,),
        out_shape=bf_shape(half, D),
        in_specs=[
            across(taken_rows), across(taken_rows),
            pl.BlockSpec((1, half, taken_rows), lambda i: (0, 0, 0)), fixed(half, taken_rows),
        ],
        out_specs=across(half),
        name="down_terms",
        **local(4 * 10**9),
    )(grads, other_grads, products, other_products)
    down, all_rows, near_terms = lax.optimization_barrier((down, all_rows, near_terms))
    down = lax.psum_scatter(
        down, "dp", scatter_dimension=0, tiled=True, axis_index_groups=X_GROUPS
    )

    kept, given = pl.pallas_call(
        gate_up_kernel,
        grid=(FOLDS,),
        out_shape=(bf_shape(2 * PART, D), bf_shape(2 * PART, D)),
        in_specs=[
            fixed(*term_shape),
            pl.BlockSpec((4, taken_rows, WIDE), lambda i: (0, 0, i)),
        ],
        out_specs=(across(2 * PART), across(2 * PART)),
        name="gate_up_terms",
        **local(4 * 10**9),
    )(near_terms, all_rows)
    taken = over_pair(given)
    echo, kept = lax.optimization_barrier((echo, kept))
    kept_scratch = [
        pltpu.VMEM((KEYS, 2 * HEAD_SIZE), BF),
        pltpu.VMEM((HEAD_SIZE, KEYS), BF),
        pltpu.VMEM((2 * ROWS, ROWS), BF),
        pltpu.VMEM((KEYS, HEAD_SIZE), F32),
        pltpu.VMEM((KEYS, HEAD_SIZE), F32),
    ]
    first_query, first_kv, grad_mixed = pl.pallas_call(
        first_backward_kernel,
        out_shape=(bf_shape(ROWS, D // 2), bf_shape(KEYS, 2 * HEAD_SIZE), bf_shape(ROWS, D)),
        in_specs=in_vmem(10),
        out_specs=tuple(in_vmem(3)),
        scratch_shapes=[*kept_scratch, pltpu.VMEM((SLOTS * CAP, D), BF)],
        name="attention_grads_0",
        **local(2 * 10**10),
    )(query[0], whole, hidden, ids, named, gain, mixed, spread, upstream[0], echo)
    blocks = (N_CTX, ROWS, 2 * HEAD_SIZE)
    slots = pltpu.VMEM((groups, N_CHIP, ROWS, 2 * HEAD_SIZE), BF)
    dmas = pltpu.SemaphoreType.DMA((groups, N_CHIP))
    d_query, d_key, d_value = pl.pallas_call(
        second_backward_kernel,
        out_shape=(bf_shape(ROWS, D), *[bf_shape(ROWS, groups * HEAD_SIZE)] * 2),
        in_specs=in_vmem(8),
        out_specs=tuple(in_vmem(3)),
        scratch_shapes=[
            *kept_scratch, pltpu.VMEM(blocks, BF), slots, slots, slots, dmas, dmas, dmas, dmas,
        ],
        compiler_params=pltpu.CompilerParams(
            collective_id=2, has_side_effects=True, vmem_limit_bytes=VMEM_LIMIT
        ),
        cost_estimate=pl.CostEstimate(flops=2 * 10**10, bytes_accessed=2**26, transcendentals=0),
        name="attention_grads_1",
    )(
        query[0], whole, hidden, mixed, spread, grad_mixed, first_query, first_kv.reshape(blocks)
    )
    expert_grads = pl.pallas_call(
        finish_kernel, out_shape=bf_shape(3, PART, D), in_specs=in_vmem(3),
        out_specs=in_vmem(1)[0], name="expert_grads", **local(10**7),
    )(kept, taken, down)
    return (
        d_query[None],
        d_key[None],
        d_value[None],
        expert_grads.transpose(1, 0, 2)[None],
    )


def solution(mesh):
    in_specs = (
        P("dp", "ctx", None),
        P("dp", "ctx", None),
        P("dp", "ctx", None),
        P("dp", None),
        P("dp", "ctx", None),
        P("dp", "ctx", None),
        P(),
        P(),
        P("dp", "ctx", None),
        P("ctx", None, None, None),
    )
    out_specs = (
        P("dp", "ctx", None),
        P("dp", "ctx", None),
        P("dp", "ctx", None),
        P("ctx", "dp", None, None),
    )
    return jax.shard_map(
        per_device, mesh=mesh, in_specs=in_specs, out_specs=out_specs, check_vma=False
    )
```
